256 devices in a mesh: row: 16 (over y_lo, z), col: 16 (over x, y_hi, core).
Axes of the slice: x: 4, y: 4 (y_hi: 2, y_lo: 2; y = y_hi * 2 + y_lo), z: 8, core: 2. Of those that a mesh axis runs over, the one named last changes fastest.
Arguments:
- amplitudes: bfloat16 [6400, 200704], P('row', 'col'), may hold values from -6 to 6
- integrals: bfloat16 [1024, 200704], P('row', 'col'), may hold values from -0.01953125 to 0.01953125
- residual_in: float32 [1024, 6400], P('col', 'row'), may hold values from -6 to 6
Outputs:
- residual_out: float32 [1024, 6400], P('col', 'row')
The draws below stay inside these ranges and needn't reach their ends.
All inputs are finite; a program needn't handle non-finite values.
Results may differ from the reference program's by a relative error of at most 0.0003.
Values may be sent and summed in bfloat16 or wider, within the bound.
A program may use at most 128 MiB of HBM per device.

```python
import jax
import jax.numpy as jnp
from jax import lax

NOCC = 80
AB = 1024
PAIRS = 6400
VPAIRS = 200704


def strengthened(entries, key, source, target, parts, factor):
    owner, partner = [(jnp.arange(entries.shape[axis_at]) // (entries.shape[axis_at] // parts)).reshape([-1 if axis == axis_at else 1 for axis in range(entries.ndim)]) for axis_at in (source, target)]
    chosen = jax.random.permutation(key, parts)[partner]
    strong = (owner == chosen) | (owner == (partner + parts // 2) % parts)
    return jnp.where(strong, factor * entries, entries)


def block_scale(rng, shape, cuts, low, top_value):
    def one(axis_at, shards_of):
        draws = jax.random.uniform(jax.random.fold_in(jax.random.fold_in(rng, 6), axis_at), (shards_of,), jnp.float32, low / len(cuts), top_value / len(cuts))
        return jnp.repeat(jnp.exp(draws), shape[axis_at] // shards_of).reshape((-1,) + (1,) * (len(shape) - axis_at - 1))

    gain = one(*cuts[0])
    for cut in cuts[1:]:
        gain = gain * one(*cut)
    return gain


def scatter_about(key, extent, deviation, most, cuts=(), held_as=jnp.bfloat16):
    loudness = block_scale(key, extent, cuts, -0.22, 0.18) if cuts else 1.0
    array = jax.random.normal(key, extent, jnp.float32) * deviation * loudness
    return jnp.minimum(jnp.maximum(array, -most), most).astype(held_as)


def heavy_noise(key, shape, scale, reach, cuts, heavy, kind=jnp.bfloat16):
    values = scale * jax.random.normal(key, shape, jnp.float32)
    if cuts:
        values = values * block_scale(key, shape, cuts, -0.22, 0.18)
    return jnp.clip(strengthened(values, jax.random.fold_in(key, 3), *heavy), -reach, reach).astype(kind)


def setup_inputs(seed: int = 0) -> dict:
    streams_of = jax.random.split(jax.random.key(seed), 4)
    amplitudes = scatter_about(streams_of[0], (PAIRS, VPAIRS), 1.0, 6.0, ((0, 16), (1, 16)))
    integrals = heavy_noise(streams_of[1], (AB, VPAIRS), VPAIRS ** -0.5, 0.01953125, ((0, 16), (1, 16)), (1, 0, 16, 2.0))
    residual_in = scatter_about(streams_of[2], (AB, PAIRS), 1.0, 6.0, ((0, 16), (1, 16)), jnp.float32)
    return {"amplitudes": amplitudes, "integrals": integrals, "residual_in": residual_in}


def reference(amplitudes, integrals, residual_in):
    ladder = lax.dot_general(integrals, amplitudes, (((1,), (1,)), ((), ())), preferred_element_type=jnp.float32)
    folded = ladder.reshape(AB, NOCC, NOCC)
    swapped = jnp.transpose(folded, (0, 2, 1)).reshape(AB, PAIRS)
    rolled = jnp.roll(swapped, AB // 2, axis=0)
    return residual_in + ladder + rolled
```

```python
import jax
import jax.numpy as jnp
from jax import lax
from jax.experimental import pallas as pl
from jax.experimental.pallas import tpu as pltpu
from jax.sharding import PartitionSpec as P

MESH = pl.DeviceIdType.MESH
NT = (((1,), (1,)), ((), ()))
RING = 8
BLOCK = 64
OCC = 5
NOCC = 80
HALF_J = 40
SUB = 2
STEPS = 7


def differs(a, b):
    return a + b - 2 * a * b


def kernel(
    amp, integ, out, own_a, far_a, ints, own_c, far_c, from_core, from_x, to_y, from_y,
    to_mirror, from_mirror, whole, from_half,
    local_sem, iy_s, iy_r, ay_s, ay_r, up_s, up_r, dn_s, dn_r, c_s, c_r, x_s, x_r, y_s, y_r, m_s, m_r, d_s, d_r,
):
    row, col = lax.axis_index("row"), lax.axis_index("col")
    y, z = row // RING, row % RING
    hx, zx, yh, core = col // 8, (col // 4) % 2, (col // 2) % 2, col % 2
    half = integ.shape[1] // 2
    mine = pl.ds(pl.multiple_of(y * half, 128), half)
    theirs = pl.ds(pl.multiple_of((1 - y) * half, 128), half)

    def dev(y_=y, z_=z, hx_=hx, zx_=zx, yh_=yh, core_=core):
        return (y_ * RING + z_, hx_ * 8 + zx_ * 4 + yh_ * 2 + core_)

    def group(distance):
        return (z + distance + RING) % RING

    def remote(src, dst, send, recv, device):
        return pltpu.make_async_remote_copy(
            src_ref=src, dst_ref=dst, send_sem=send, recv_sem=recv, device_id=device, device_id_type=MESH
        )

    barrier = pltpu.get_barrier_semaphore()

    def greet(device):
        pl.semaphore_signal(barrier, inc=1, device_id=device, device_id_type=MESH)

    near = [dev(y_=1 - y), dev(z_=group(1)), dev(z_=group(-1)), dev(core_=1 - core), dev(zx_=1 - zx), dev(hx_=1 - hx)]
    near += [dev(zx_=1 - zx, hx_=1 - hx), dev(yh_=1 - yh), dev(yh_=1 - yh, y_=1 - y)]
    for device in near:
        greet(device)

    def is_me(h, y_, z_):
        return jnp.logical_and(jnp.logical_and(h == hx, y_ == y), z_ == z)

    def greet_source(r, _):
        @pl.when(jnp.logical_not(is_me(y, r // RING, r % RING)))
        def _():
            greet(dev(hx_=y, y_=r // RING, z_=r % RING))

        return 0

    lax.fori_loop(0, 2 * RING, greet_source, 0)
    pl.semaphore_wait(barrier, len(near) + 2 * RING - (1 - differs(hx, y)))

    def rows_of(owner_y, u):
        return pl.ds(pl.multiple_of(owner_y * BLOCK + u * (BLOCK // SUB), BLOCK // SUB), BLOCK // SUB)

    def sub(u):
        return pl.ds(u * (BLOCK // SUB), BLOCK // SUB)

    def up(m, u, first=False):
        place = ints.at[group(-(m // 2)), rows_of(y if m % 2 == 0 else 1 - y, u)]
        src = integ.at[sub(u), mine] if first else place
        return remote(src, place, up_s.at[m, u], up_r.at[m, u], dev(z_=group(1)))

    def down(m, u, first=False):
        place = ints.at[group(3 if m == 6 else m // 2), rows_of(y if m % 2 == 0 and m < 6 else 1 - y, u)]
        src = integ.at[sub(u), mine] if first else place
        return remote(src, place, dn_s.at[m, u], dn_r.at[m, u], dev(z_=group(-1)))

    def up_arrives(n, u):
        place = ints.at[group(-1 - n // 2), rows_of(y if n % 2 == 0 else 1 - y, u)]
        remote(place, place, up_s.at[n, u], up_r.at[n, u], dev(z_=group(1))).wait_recv()

    def down_arrives(n, u):
        place = ints.at[group(4 if n == 6 else 1 + n // 2), rows_of(y if n % 2 == 0 and n < 6 else 1 - y, u)]
        remote(place, place, dn_s.at[n, u], dn_r.at[n, u], dev(z_=group(-1))).wait_recv()

    def swap_i(u):
        return remote(integ.at[sub(u), theirs], ints.at[z, rows_of(y, u)], iy_s.at[u], iy_r.at[u], dev(y_=1 - y))

    def swap_i_arrives(u):
        place = ints.at[z, rows_of(1 - y, u)]
        remote(place, place, iy_s.at[u], iy_r.at[u], dev(y_=1 - y)).wait_recv()

    def swap_a(i):
        part = pl.ds(i * NOCC, NOCC)
        return remote(amp.at[part, theirs], far_a.at[part], ay_s.at[i], ay_r.at[i], dev(y_=1 - y))

    for u in range(SUB):
        swap_i(u).start()
        up(0, u, True).start()
        down(0, u, True).start()
    load_i = pltpu.make_async_copy(integ.at[:, mine], ints.at[z, pl.ds(pl.multiple_of(y * BLOCK, BLOCK), BLOCK)], local_sem.at[0])
    load_a = pltpu.make_async_copy(amp.at[:, mine], own_a, local_sem.at[1])
    load_i.start()
    load_a.start()
    for u in range(SUB):
        swap_i_arrives(u)
        up(1, u).start()
        down(1, u).start()
        if u == 0:
            swap_a(0).start()
    swap_a(1).start()
    load_i.wait()
    load_a.wait()

    def own_product(g):
        value = lax.dot_general(own_a[...], ints[g], NT, preferred_element_type=jnp.float32)
        own_c[g] = value.reshape(OCC, NOCC, 2 * BLOCK)

    def far_product(i, count, g):
        at = pl.ds(i * NOCC, count * NOCC)
        value = lax.dot_general(far_a[at, :], ints[g], NT, preferred_element_type=jnp.float32)
        far_c[g, pl.ds(i, count)] = value.reshape(count, NOCC, 2 * BLOCK)

    def over(first, count, act):
        lax.fori_loop(0, count, lambda t, _: (act(group(first + t)), 0)[1], 0)

    def part_of(role):
        return pl.ds(0, OCC) if role == 0 else pl.ds(0, OCC - 1) if role == 1 else pl.ds(OCC - 1, 1)

    def held(role):
        return own_c if role == 0 else far_c

    def to_core(g, role):
        at = part_of(role)
        return remote(
            held(role).at[g, at], from_core.at[g // 2, min(role, 1), at], c_s.at[g // 2, role], c_r.at[g // 2, role], dev(core_=1 - core)
        )

    def to_x(g, role, h, act):
        at = part_of(role)
        z2, z1 = g // 4, (g // 2) % 2
        delta = 2 * differs(h, hx) + differs(z2, zx)

        @pl.when(delta > 0)
        def _():
            act(
                remote(
                    held(role).at[g, at, pl.ds(h * HALF_J, HALF_J)], from_x.at[delta - 1, z1, min(role, 1), at],
                    x_s.at[g // 2, role, h], x_r.at[delta - 1, z1, role], dev(hx_=h, zx_=z2),
                )
            )

    def reduce_core(g, role):
        @pl.when(g % 2 != core)
        def _():
            to_core(g, role).start()

    def reduce_x(g, role):
        @pl.when(g % 2 == core)
        def _():
            to_core(g, role).wait_recv()
            at = part_of(role)
            held(role)[g, at] += from_core[g // 2, min(role, 1), at]
            for h in range(2):
                to_x(g, role, h, lambda copy: copy.start())

    own_product(z)
    reduce_core(z, 0)
    for n in range(STEPS):
        for u in range(SUB):
            up_arrives(n, u)
            if n + 2 < STEPS:
                up(n + 2, u).start()
            down_arrives(n, u)
            if n + 2 < STEPS - 1:
                down(n + 2, u).start()
            elif n == STEPS - 2:
                down(n + 1, u).start()
        if n in (1, 2, 3):
            swap_a(n + 1).start()
        if n == 0:
            reduce_x(z, 0)
        elif n in (1, 3, 5):
            d = (n + 1) // 2
            for sign in (1, -1):
                own_product(group(sign * d))
                reduce_core(group(sign * d), 0)
            for sign in (1, -1):
                reduce_x(group(sign * d), 0)
        if n == 2:
            swap_a(0).wait_recv()
            over(-1, 3, lambda g: far_product(0, 1, g))
        elif n == 3:
            for sign in (2, -2):
                far_product(0, 1, group(sign))
            swap_a(1).wait_recv()
            over(-2, 5, lambda g: far_product(1, 1, g))
        elif n == 4:
            swap_a(2).wait_recv()
            over(-2, 5, lambda g: far_product(2, 1, g))
        elif n == 5:
            for sign in (3, -3):
                far_product(0, 3, group(sign))
            swap_a(3).wait_recv()
            over(-3, 7, lambda g: far_product(3, 1, g))
            over(-3, 7, lambda g: reduce_core(g, 1))
            over(-3, 7, lambda g: reduce_x(g, 1))
    last = group(4)
    own_product(last)
    reduce_core(last, 0)
    far_product(0, 4, last)
    reduce_core(last, 1)
    reduce_x(last, 0)
    reduce_x(last, 1)
    swap_a(4).wait_recv()
    for b in range(2):
        four = ints[pl.ds(4 * b, 4)].reshape(4 * 2 * BLOCK, half)
        value = lax.dot_general(far_a[pl.ds(4 * NOCC, NOCC), :], four, NT, preferred_element_type=jnp.float32)
        for q in range(4):
            far_c[4 * b + q, 4] = value[:, q * 2 * BLOCK : (q + 1) * 2 * BLOCK]
    over(0, RING, lambda g: reduce_core(g, 2))
    over(0, RING, lambda g: reduce_x(g, 2))

    j_mine = pl.ds(pl.multiple_of(hx * HALF_J, 8), HALF_J)

    def x_sum(z1, far):
        g = zx * 4 + z1 * 2 + core
        for role in (1, 2) if far else (0,):
            for delta in range(3):
                at = part_of(role)
                place = from_x.at[delta, z1, far, at]
                remote(place, place, x_s.at[0, role, 0], x_r.at[delta, z1, role], dev(hx_=1 - hx)).wait_recv()
        total = held(far)[g, :, j_mine, :]
        for delta in range(3):
            total = total + from_x[delta, z1, far]
        return total

    def y_copy(e):
        target = dev(yh_=1 - yh if e & 2 else yh, y_=1 - y if e & 1 else y)
        return remote(to_y.at[e - 1], from_y.at[e - 1], y_s.at[e - 1], y_r.at[e - 1], target)

    for e in (2, 3, 1):
        to_y[e - 1] = x_sum(1 - yh if e & 2 else yh, e & 1)
        y_copy(e).start()
    total = x_sum(yh, 0)
    for e in (2, 3, 1):
        y_copy(e).wait_recv()
        total = total + from_y[e - 1]

    whole[:, j_mine, :] = total
    mirror = dev(hx_=1 - hx)
    keep = whole.at[:, j_mine]
    j_theirs = pl.ds(pl.multiple_of((1 - hx) * HALF_J, 8), HALF_J)
    direct = remote(keep, from_half, d_s, d_r, mirror)
    direct.start()
    for t in range(RING):
        for b in range(OCC):
            to_mirror[t, b, pl.ds(0, OCC), :] = total[:, t * OCC + b, :]

    def mirror_copy(t, h):
        return remote(to_mirror.at[t], from_mirror.at[row], m_s.at[t, h], m_r.at[row], dev(hx_=h, y_=hx, z_=t))

    def each_mirror(act):
        def body(t, _):
            for h in range(2):

                @pl.when(jnp.logical_not(is_me(h, hx, t)))
                def _():
                    act(t, h)

            return 0

        lax.fori_loop(0, RING, body, 0)

    each_mirror(lambda t, h: mirror_copy(t, h).start())

    @pl.when(hx == y)
    def _():
        from_mirror[row] = to_mirror[z]

    def mirror_arrives(r, _):
        @pl.when(jnp.logical_not(is_me(y, r // RING, r % RING)))
        def _():
            place = from_mirror.at[r]
            remote(place, place, m_s.at[0, 0], m_r.at[r], mirror).wait_recv()

        return 0

    lax.fori_loop(0, 2 * RING, mirror_arrives, 0)
    direct.wait()
    whole[:, j_theirs, :] = from_half[...]
    for r in range(2 * RING):
        at = pl.ds(r * OCC, OCC)
        turned = pltpu.roll(from_mirror[r].reshape(OCC * 8, 2 * BLOCK), BLOCK, 1).reshape(OCC, 8, 2 * BLOCK)
        whole[:, at, :] += turned[:, :OCC, :]

    @pl.when(hx == 0)
    def _():
        out[...] = whole[...]

    @pl.when(hx == 1)
    def _():
        out[...] = pltpu.roll(whole[...].reshape(OCC * NOCC, 2 * BLOCK), BLOCK, 1).reshape(OCC, NOCC, 2 * BLOCK)

    for u in range(SUB):
        swap_i(u).wait_send()
        for m in range(STEPS):
            up(m, u, m == 0).wait_send()
            down(m, u, m == 0).wait_send()
    for i in range(OCC):
        swap_a(i).wait_send()

    def sums_sent(g2, _):
        for role in range(3):
            to_core(2 * g2 + 1 - core, role).wait_send()
            for h in range(2):
                to_x(2 * g2 + core, role, h, lambda copy: copy.wait_send())
        return 0

    lax.fori_loop(0, RING // 2, sums_sent, 0)
    for e in (2, 3, 1):
        y_copy(e).wait_send()
    each_mirror(lambda t, h: mirror_copy(t, h).wait_send())


def on_device(amplitudes, integrals, residual_in):
    pairs, depth = amplitudes.shape
    half = depth // 2
    bf16, f32, lanes = jnp.bfloat16, jnp.float32, 2 * BLOCK
    dma = pltpu.SemaphoreType.DMA
    ladder = pl.pallas_call(
        kernel,
        out_shape=jax.ShapeDtypeStruct((OCC, NOCC, lanes), f32),
        in_specs=[pl.BlockSpec(memory_space=pltpu.HBM)] * 2,
        out_specs=pl.BlockSpec(memory_space=pltpu.VMEM),
        scratch_shapes=[
            pltpu.VMEM((pairs, half), bf16),
            pltpu.VMEM((pairs, half), bf16),
            pltpu.VMEM((RING, lanes, half), bf16),
            pltpu.VMEM((RING, OCC, NOCC, lanes), f32),
            pltpu.VMEM((RING, OCC, NOCC, lanes), f32),
            pltpu.VMEM((RING // 2, 2, OCC, NOCC, lanes), f32),
            pltpu.VMEM((3, 2, 2, OCC, HALF_J, lanes), f32),
            pltpu.VMEM((3, OCC, HALF_J, lanes), f32),
            pltpu.VMEM((3, OCC, HALF_J, lanes), f32),
            pltpu.VMEM((RING, OCC, 8, lanes), f32),
            pltpu.VMEM((2 * RING, OCC, 8, lanes), f32),
            pltpu.VMEM((OCC, NOCC, lanes), f32),
            pltpu.VMEM((OCC, HALF_J, lanes), f32),
            dma((2,)),
            dma((SUB,)),
            dma((SUB,)),
            dma((OCC,)),
            dma((OCC,)),
            dma((STEPS, SUB)),
            dma((STEPS, SUB)),
            dma((STEPS, SUB)),
            dma((STEPS, SUB)),
            dma((RING // 2, 3)),
            dma((RING // 2, 3)),
            dma((RING // 2, 3, 2)),
            dma((3, 2, 3)),
            dma((3,)),
            dma((3,)),
            dma((RING, 2)),
            dma((2 * RING,)),
            dma,
            dma,
        ],
        compiler_params=pltpu.CompilerParams(
            collective_id=0, has_side_effects=True, vmem_limit_bytes=48 * 1024 * 1024
        ),
        cost_estimate=pl.CostEstimate(
            flops=2 * pairs * depth * 16 * BLOCK, bytes_accessed=4 * pairs * depth, transcendentals=0
        ),
        name="ladder",
    )(amplitudes, integrals)
    return residual_in + ladder.reshape(pairs, lanes)[:, :BLOCK].T


def solution(mesh):
    placed = (P("row", "col"), P("row", "col"), P("col", "row"))
    return jax.shard_map(
        on_device, mesh=mesh, in_specs=placed, out_specs=P("col", "row"), check_vma=False
    )
```

```python
import jax
import jax.numpy as jnp
from jax import lax
from jax.experimental import pallas as pl
from jax.experimental.pallas import tpu as pltpu
from jax.sharding import PartitionSpec as P

MESH = pl.DeviceIdType.MESH
NT = (((1,), (1,)), ((), ()))
RING = 8
BLOCK = 64
OCC = 5
NOCC = 80
HALF_J = 40
SUB = 2
STEPS = 7
LANES = 2 * BLOCK
CUTS = (0, 16, 32, 41, 49)


def differs(a, b):
    return a + b - 2 * a * b


def kernel(
    amp, integ, out, rows_a, ints, sums, from_core, from_x, late_in, from_all, to_y, from_y,
    total, to_mirror, from_mirror, to_late, from_late, direct_half, turned, upright,
    local_sem, iy_s, iy_r, ay_s, ay_r, al_s, al_r, up_s, up_r, dn_s, dn_r, c_s, c_r, x_s, x_r, lc_s, lc_r, all_s, all_r,
    y_s, y_r, m_s, m_r, lm_s, lm_r, d_s, d_r,
):
    row, col = lax.axis_index("row"), lax.axis_index("col")
    y, z = row // RING, row % RING
    hx, zx, yh, core = col // 8, (col // 4) % 2, (col // 2) % 2, col % 2
    half = integ.shape[1] // 2
    mine = pl.ds(pl.multiple_of(y * half, 128), half)
    theirs = pl.ds(pl.multiple_of((1 - y) * half, 128), half)
    cuts = [(128 * a, 128 * (b - a)) for a, b in zip(CUTS[:-1], CUTS[1:])]

    def dev(y_=y, z_=z, hx_=hx, zx_=zx, yh_=yh, core_=core):
        return (y_ * RING + z_, hx_ * 8 + zx_ * 4 + yh_ * 2 + core_)

    def group(distance):
        return (z + distance + RING) % RING

    def slot(d):
        return (d % 2) * 4 + d // 2

    def remote(src, dst, send, recv, device):
        return pltpu.make_async_remote_copy(
            src_ref=src, dst_ref=dst, send_sem=send, recv_sem=recv, device_id=device, device_id_type=MESH
        )

    barrier = pltpu.get_barrier_semaphore()

    def greet(device):
        pl.semaphore_signal(barrier, inc=1, device_id=device, device_id_type=MESH)

    near = [dev(z_=group(1)), dev(z_=group(-1)), dev(core_=1 - core), dev(yh_=1 - yh)]
    near += [dev(zx_=1 - zx), dev(hx_=1 - hx), dev(zx_=1 - zx, hx_=1 - hx)]
    for device in near:
        greet(device)

    def is_me(h, y_, z_):
        return jnp.logical_and(jnp.logical_and(h == hx, y_ == y), z_ == z)

    def greet_source(t, _):
        greet(((1 - y) * RING + z, 2 * t + core))
        for y_ in range(2):

            @pl.when(jnp.logical_not(is_me(y, y_, t)))
            def _(y_=y_):
                greet(dev(hx_=y, y_=y_, z_=t))

        return 0

    lax.fori_loop(0, RING, greet_source, 0)
    pl.semaphore_wait(barrier, len(near) + 3 * RING - (1 - differs(hx, y)))

    upright[pl.ds(OCC * NOCC, 4 * LANES - OCC * NOCC), :] = jnp.zeros((4 * LANES - OCC * NOCC, LANES), jnp.float32)

    def cut_along_q(m):
        return m >= STEPS - 2

    def pieces(m):
        return range(len(cuts) if cut_along_q(m) else SUB)

    def block_at(distance, owner_y, m, u):
        if cut_along_q(m):
            start, size, columns = 0, BLOCK, pl.ds(*cuts[u])
        else:
            start, size, columns = u * (BLOCK // SUB), BLOCK // SUB, pl.ds(0, half)
        start = pl.multiple_of(owner_y * BLOCK + start, BLOCK // SUB)
        return ints.at[slot(distance % RING), pl.ds(start, size), columns]

    def sub(u):
        return pl.ds(u * (BLOCK // SUB), BLOCK // SUB)

    def up_block(m):
        return -(m // 2), y if m % 2 == 0 else 1 - y

    def down_block(m):
        return (0, 0, 1, 1, 2, 2, 3)[m], (y, 1 - y, y, 1 - y, 1 - y, y, 1 - y)[m]

    def up(m, u):
        distance, owner = up_block(m)
        src = integ.at[sub(u), mine] if m == 0 else block_at(distance, owner, m, u)
        return remote(src, block_at(distance - 1, owner, m, u), up_s.at[m, u], up_r.at[m, u], dev(z_=group(1)))

    def down(m, u):
        distance, owner = down_block(m)
        src = integ.at[sub(u), mine] if m == 0 else block_at(distance, owner, m, u)
        return remote(src, block_at(distance + 1, owner, m, u), dn_s.at[m, u], dn_r.at[m, u], dev(z_=group(-1)))

    def up_arrives(n, u):
        distance, owner = up_block(n)
        place = block_at(distance - 1, owner, n, u)
        remote(place, place, up_s.at[n, u], up_r.at[n, u], dev(z_=group(1))).wait_recv()

    def down_arrives(n, u):
        distance, owner = down_block(n)
        place = block_at(distance + 1, owner, n, u)
        remote(place, place, dn_s.at[n, u], dn_r.at[n, u], dev(z_=group(-1))).wait_recv()

    def swap_i(u):
        return remote(integ.at[sub(u), theirs], block_at(0, y, 0, u), iy_s.at[u], iy_r.at[u], dev(y_=1 - y))

    def swap_i_arrives(u):
        place = block_at(0, 1 - y, 0, u)
        remote(place, place, iy_s.at[u], iy_r.at[u], dev(y_=1 - y)).wait_recv()

    def swap_a(i):
        src, dst = amp.at[pl.ds(i * NOCC, NOCC), theirs], rows_a.at[pl.ds((OCC + i) * NOCC, NOCC)]
        return remote(src, dst, ay_s.at[i], ay_r.at[i], dev(y_=1 - y))

    def swap_cut(i, k):
        start, width = cuts[k]
        src = amp.at[pl.ds(i * NOCC, NOCC), pl.ds(pl.multiple_of((1 - y) * half + start, 128), width)]
        dst = rows_a.at[pl.ds((OCC + i) * NOCC, NOCC), pl.ds(start, width)]
        return remote(src, dst, al_s.at[i - OCC + 2, k], al_r.at[i - OCC + 2, k], dev(y_=1 - y))

    for u in range(SUB):
        swap_i(u).start()
        up(0, u).start()
        down(0, u).start()
    own_rows = pl.ds(pl.multiple_of(y * BLOCK, BLOCK), BLOCK)
    load_i = pltpu.make_async_copy(integ.at[:, mine], ints.at[slot(0), own_rows], local_sem.at[0])
    load_a = pltpu.make_async_copy(amp.at[:, mine], rows_a.at[pl.ds(0, OCC * NOCC)], local_sem.at[1])
    load_i.start()
    load_a.start()
    for u in range(SUB):
        swap_i_arrives(u)
        up(1, u).start()
        down(1, u).start()
        if u == 0:
            swap_a(0).start()
    swap_a(1).start()
    load_i.wait()
    load_a.wait()

    def product(first, count, at, blocks, k=None):
        columns, width = (pl.ds(0, half), half) if k is None else (pl.ds(*cuts[k]), cuts[k][1])
        value = lax.dot_general(
            rows_a[pl.ds(first * NOCC, count * NOCC), columns],
            ints[pl.ds(at, blocks), :, columns].reshape(blocks * LANES, width),
            NT,
            preferred_element_type=jnp.float32,
        )
        for q in range(blocks):
            part = value[:, q * LANES : (q + 1) * LANES].reshape(count, NOCC, LANES)
            if k is None or k == 0:
                sums[at + q, pl.ds(first, count)] = part
            else:
                sums[at + q, pl.ds(first, count)] += part

    def five_blocks(first, k=None):
        product(first, 1, slot(0), 2, k)
        product(first, 1, slot(6), 2, k)
        product(first, 1, slot(7), 1, k)

    def part_of(role):
        return (pl.ds(0, OCC), pl.ds(OCC, OCC - 2), pl.ds(2 * OCC - 2, 1), pl.ds(0, 2 * OCC - 1))[role]

    def is_kept(d):
        return group(d) % 2 == core

    def to_core(d, role):
        at = part_of(role)
        return remote(
            sums.at[slot(d), at], from_core.at[d // 2, at], c_s.at[d // 2, role % 3], c_r.at[d // 2, role % 3], dev(core_=1 - core)
        )

    def to_x(d, role, h, act):
        at, g = part_of(role), group(d)
        z2, z1 = g // 4, (g // 2) % 2
        delta = 2 * differs(h, hx) + differs(z2, zx)

        @pl.when(delta > 0)
        def _():
            act(
                remote(
                    sums.at[slot(d), at, pl.ds(h * HALF_J, HALF_J)], from_x.at[delta - 1, z1, at],
                    x_s.at[d // 2, role % 3, h], x_r.at[delta - 1, z1], dev(hx_=h, zx_=z2),
                )
            )

    def reduce_core(d, role):
        @pl.when(jnp.logical_not(is_kept(d)))
        def _():
            to_core(d, role).start()

    def reduce_x(d, role):
        @pl.when(is_kept(d))
        def _():
            to_core(d, role).wait_recv()
            at = part_of(role)
            sums[slot(d), at] += from_core[d // 2, at]
            for h in range(2):
                to_x(d, role, h, lambda copy: copy.start())

    def over_five(act):
        lax.fori_loop(0, 5, lambda t, _: (act(t + 3 * (t // 3)), 0)[1], 0)

    last = group(4)
    j_mine = pl.ds(pl.multiple_of(hx * HALF_J, 8), HALF_J)
    j_theirs = pl.ds(pl.multiple_of((1 - hx) * HALF_J, 8), HALF_J)
    most = pl.ds(0, OCC - 1)

    def unit(z1):
        return zx * 4 + z1 * 2 + core

    def kept_of(far):
        return most if far else pl.ds(0, OCC)

    def x_arrives(z1):
        for delta in range(3):
            place = from_x.at[delta, z1]
            remote(place, place, x_s.at[0, 0, 0], x_r.at[delta, z1], dev(hx_=1 - hx)).wait_recv()

    def x_sum(z1, far):
        at = pl.ds(OCC, OCC - 1) if far else pl.ds(0, OCC)
        value = sums[slot((unit(z1) - z + RING) % RING), at, j_mine, :]
        for delta in range(3):
            value = value + from_x[delta, z1, at]
        return value

    def y_copy(e):
        at = kept_of(e & 1)
        target = dev(yh_=1 - yh if e & 2 else yh, y_=1 - y if e & 1 else y)
        return remote(to_y.at[e - 1, at], from_y.at[e - 1, at], y_s.at[e - 1], y_r.at[e - 1], target)

    def y_send(e):
        to_y[e - 1, kept_of(e & 1)] = x_sum(1 - yh if e & 2 else yh, e & 1)
        y_copy(e).start()

    def y_stage(ready):
        @pl.when(ready(unit(1 - yh)))
        def _():
            x_arrives(1 - yh)
            y_send(2)
            y_send(3)

        @pl.when(ready(unit(yh)))
        def _():
            x_arrives(yh)
            y_send(1)
            total[...] = x_sum(yh, 0)

    mirror = dev(hx_=1 - hx)

    def direct(k):
        at = pl.ds(OCC - 1, 1) if k else most
        return remote(total.at[at], direct_half.at[at], d_s.at[k], d_r.at[k], mirror)

    def mirror_copy(k, t, h):
        src, dst, send, recv = ((to_mirror, from_mirror, m_s, m_r), (to_late, from_late, lm_s, lm_r))[k]
        return remote(src.at[t], dst.at[row], send.at[t, h], recv.at[row], dev(hx_=h, y_=hx, z_=t))

    def each_mirror(act):
        def body(t, _):
            for h in range(2):

                @pl.when(jnp.logical_not(is_me(h, hx, t)))
                def _():
                    act(t, h)

            return 0

        lax.fori_loop(0, RING, body, 0)

    def mirror_arrives(k):
        dst, send, recv = ((from_mirror, m_s, m_r), (from_late, lm_s, lm_r))[k]

        def body(r, _):
            @pl.when(jnp.logical_not(is_me(y, r // RING, r % RING)))
            def _():
                place = dst.at[r]
                remote(place, place, send.at[0, 0], recv.at[r], mirror).wait_recv()

            return 0

        lax.fori_loop(0, 2 * RING, body, 0)

    def mirror_stage(ready):
        @pl.when(ready(unit(yh)))
        def _():
            for e in (2, 3, 1):
                y_copy(e).wait_recv()
            total[...] += from_y[1]
            total[most] += from_y[0, most] + from_y[2, most]
            direct(0).start()
            for t in range(RING):
                for b in range(OCC):
                    to_mirror[t, pl.ds(b * 4, 4), :] = total[most, t * OCC + b, :]
            each_mirror(lambda t, h: mirror_copy(0, t, h).start())

            @pl.when(hx == y)
            def _():
                from_mirror[row] = to_mirror[z]

    kept = (z + core) % 2
    late_core = remote(
        sums.at[pl.ds(4 * (1 - kept), 4), 2 * OCC - 1], late_in, lc_s, lc_r, dev(core_=1 - core)
    )

    def to_owner(q, h):
        d = 2 * q + kept
        src = sums.at[slot(d), 2 * OCC - 1, pl.ds(h * HALF_J, HALF_J)]
        owner = h * RING + group(d)
        return remote(src, from_all.at[col // 2], all_s.at[q, h], all_r.at[col // 2], ((1 - y) * RING + z, owner))

    def each_owner(act):
        def body(q, _):
            for h in range(2):
                act(to_owner(q, h))
            return 0

        lax.fori_loop(0, RING // 2, body, 0)

    product(0, OCC, slot(0), 1)
    reduce_core(0, 0)
    for n in range(STEPS - 2):
        if n == 4:
            for k in pieces(5):
                down(5, k).start()
        for u in pieces(n):
            up_arrives(n, u)
            if n + 2 < STEPS - 2:
                up(n + 2, u).start()
            down_arrives(n, u)
            if n in (0, 1):
                down(n + 2, u).start()
            elif n == 3:
                down(4, u).start()
        if n == 3:
            for k in pieces(5):
                up(5, k).start()
        elif n == 4:
            for k in pieces(6):
                up(6, k).start()
                down(6, k).start()
        if n == 1:
            swap_a(2).start()
        elif n in (2, 3):
            for k in range(len(cuts)):
                swap_cut(n + 1, k).start()
        if n == 0:
            reduce_x(0, 0)
        elif n in (1, 3):
            d = (n + 1) // 2
            for distance in (d, RING - d):
                product(0, OCC + d - 1, slot(distance), 1)
                reduce_core(distance, 0)
            for distance in (d, RING - d):
                reduce_x(distance, 0)
        if n == 2:
            swap_a(0).wait_recv()
            for distance in (0, 1, 7):
                product(OCC, 1, slot(distance), 1)
        elif n == 3:
            swap_a(1).wait_recv()
            five_blocks(OCC + 1)
        elif n == 4:
            swap_a(2).wait_recv()
            five_blocks(OCC + 2)
            over_five(lambda d: reduce_core(d, 1))
            over_five(lambda d: reduce_x(d, 1))

    def ring_sent(steps):
        for m in steps:
            for u in pieces(m):
                up(m, u).wait_send()
                down(m, u).wait_send()

    def sums_sent(d, role):
        @pl.when(jnp.logical_not(is_kept(d)))
        def _():
            to_core(d, role).wait_send()

        @pl.when(is_kept(d))
        def _():
            for h in range(2):
                to_x(d, role, h, lambda copy: copy.wait_send())

    for u in range(SUB):
        swap_i(u).wait_send()
    ring_sent(range(4))
    for i in range(2):
        swap_a(i).wait_send()

    for k in range(len(cuts)):
        up_arrives(5, k)
        down_arrives(5, k)
        swap_cut(3, k).wait_recv()
        product(0, 2 * OCC - 1, slot(3), 2, k)
        five_blocks(2 * OCC - 2, k)
    for d in (3, 5):
        reduce_core(d, 3)
    over_five(lambda d: reduce_core(d, 2))
    for d in (3, 5):
        reduce_x(d, 3)
    over_five(lambda d: reduce_x(d, 2))

    ring_sent((4,))
    swap_a(2).wait_send()
    for role in range(2):
        over_five(lambda d, role=role: sums_sent(d, role))

    final = len(cuts) - 1
    for k in range(len(cuts)):
        up_arrives(6, k)
        down_arrives(6, k)
        product(0, 2 * OCC - 1, slot(4), 1, k)
        if k == final:
            reduce_core(4, 3)
        if k == final - 1:
            y_stage(lambda g: g != last)
        if k > 0:
            swap_cut(4, k - 1).wait_recv()
            product(2 * OCC - 1, 1, 0, 4, k - 1)
            product(2 * OCC - 1, 1, 4, 4, k - 1)
    reduce_x(4, 3)
    swap_cut(4, final).wait_recv()
    product(2 * OCC - 1, 1, 4 * (1 - kept), 4, final)
    late_core.start()
    product(2 * OCC - 1, 1, 4 * kept, 4, final)
    late_core.wait_recv()
    sums[pl.ds(4 * kept, 4), 2 * OCC - 1] += late_in[...]
    each_owner(lambda copy: copy.start())

    mirror_stage(lambda g: g != last)
    y_stage(lambda g: g == last)
    mirror_stage(lambda g: g == last)

    ring_sent((5, 6))
    for k in range(len(cuts)):
        swap_cut(3, k).wait_send()
        swap_cut(4, k).wait_send()
    over_five(lambda d: sums_sent(d, 2))
    for d in (3, 4, 5):
        sums_sent(d, 3)

    def late_arrives(r, _):
        place = from_all.at[r]
        remote(place, place, all_s.at[0, 0], all_r.at[r], mirror).wait_recv()
        return 0

    lax.fori_loop(0, RING, late_arrives, 0)
    value = total[OCC - 1]
    for r in range(RING):
        value = value + from_all[r]
    total[OCC - 1] = value
    for t in range(RING):
        to_late[t, pl.ds(0, OCC), :] = total[OCC - 1, pl.ds(t * OCC, OCC), :]
    each_mirror(lambda t, h: mirror_copy(1, t, h).start())
    direct(1).start()

    @pl.when(hx == y)
    def _():
        from_late[row] = to_late[z]

    mirror_arrives(0)
    for r in range(2 * RING):
        for b in range(OCC):
            turned[b, pl.ds(r * OCC, OCC - 1), :] = from_mirror[r, pl.ds(b * 4, 4), :]
    direct(0).wait_recv()

    late_core.wait_send()
    each_owner(lambda copy: copy.wait_send())
    for e in (1, 2, 3):
        y_copy(e).wait_send()
    direct(0).wait_send()
    each_mirror(lambda t, h: mirror_copy(0, t, h).wait_send())
    mirror_arrives(1)
    for r in range(2 * RING):
        turned[:, r * OCC + OCC - 1, :] = from_late[r, pl.ds(0, OCC), :]
    direct(1).wait_recv()

    def finish(straight, swapped):
        straight, swapped = (v.reshape(OCC * HALF_J, LANES) for v in (straight, swapped))
        here = jnp.where(hx == 0, straight, swapped)
        there = jnp.where(hx == 0, swapped, straight)
        value = here + pltpu.roll(there, BLOCK, 1)
        return [value[i * HALF_J : (i + 1) * HALF_J] for i in range(OCC)]

    for h, straight in ((hx, total), (1 - hx, direct_half)):
        at = pl.ds(pl.multiple_of(h * HALF_J, 8), HALF_J)
        for i, value in enumerate(finish(straight[...], turned[:, at, :])):
            upright[pl.ds(pl.multiple_of(i * NOCC + h * HALF_J, 8), HALF_J), :] = value
    out[...] = upright[...].T[:BLOCK, : OCC * NOCC]

    direct(1).wait_send()
    each_mirror(lambda t, h: mirror_copy(1, t, h).wait_send())


def on_device(amplitudes, integrals, residual_in):
    pairs, depth = amplitudes.shape
    half = depth // 2
    bf16, f32 = jnp.bfloat16, jnp.float32
    dma = pltpu.SemaphoreType.DMA
    cuts = len(CUTS) - 1
    ladder = pl.pallas_call(
        kernel,
        out_shape=jax.ShapeDtypeStruct((BLOCK, pairs), f32),
        in_specs=[pl.BlockSpec(memory_space=pltpu.HBM)] * 2,
        out_specs=pl.BlockSpec(memory_space=pltpu.VMEM),
        scratch_shapes=[
            pltpu.VMEM((2 * pairs, half), bf16),
            pltpu.VMEM((RING, LANES, half), bf16),
            pltpu.VMEM((RING, 2 * OCC, NOCC, LANES), f32),
            pltpu.VMEM((RING // 2, 2 * OCC - 1, NOCC, LANES), f32),
            pltpu.VMEM((3, 2, 2 * OCC - 1, HALF_J, LANES), f32),
            pltpu.VMEM((RING // 2, NOCC, LANES), f32),
            pltpu.VMEM((RING, HALF_J, LANES), f32),
            pltpu.VMEM((3, OCC, HALF_J, LANES), f32),
            pltpu.VMEM((3, OCC, HALF_J, LANES), f32),
            pltpu.VMEM((OCC, HALF_J, LANES), f32),
            pltpu.VMEM((RING, 24, LANES), f32),
            pltpu.VMEM((2 * RING, 24, LANES), f32),
            pltpu.VMEM((RING, 8, LANES), f32),
            pltpu.VMEM((2 * RING, 8, LANES), f32),
            pltpu.VMEM((OCC, HALF_J, LANES), f32),
            pltpu.VMEM((OCC, NOCC, LANES), f32),
            pltpu.VMEM((4 * LANES, LANES), f32),
            dma((2,)),
            dma((SUB,)),
            dma((SUB,)),
            dma((OCC - 2,)),
            dma((OCC - 2,)),
            dma((2, cuts)),
            dma((2, cuts)),
            dma((STEPS, cuts)),
            dma((STEPS, cuts)),
            dma((STEPS, cuts)),
            dma((STEPS, cuts)),
            dma((RING // 2, 3)),
            dma((RING // 2, 3)),
            dma((RING // 2, 3, 2)),
            dma((3, 2)),
            dma,
            dma,
            dma((RING // 2, 2)),
            dma((RING,)),
            dma((3,)),
            dma((3,)),
            dma((RING, 2)),
            dma((2 * RING,)),
            dma((RING, 2)),
            dma((2 * RING,)),
            dma((2,)),
            dma((2,)),
        ],
        compiler_params=pltpu.CompilerParams(
            collective_id=0, has_side_effects=True, vmem_limit_bytes=60 * 1024 * 1024
        ),
        cost_estimate=pl.CostEstimate(
            flops=2 * pairs * depth * 16 * BLOCK, bytes_accessed=4 * pairs * depth, transcendentals=0
        ),
        name="ladder",
    )(amplitudes, integrals)
    return residual_in + ladder


def solution(mesh):
    placed = (P("row", "col"), P("row", "col"), P("col", "row"))
    return jax.shard_map(
        on_device, mesh=mesh, in_specs=placed, out_specs=P("col", "row"), check_vma=False
    )
```

```python
import jax
import jax.numpy as jnp
from jax import lax
from jax.experimental import pallas as pl
from jax.experimental.pallas import tpu as pltpu
from jax.sharding import PartitionSpec as P

MESH = pl.DeviceIdType.MESH
NT = (((1,), (1,)), ((), ()))
RING = 8
BLOCK = 64
OCC = 5
NOCC = 80
HALF_J = 40
SUB = 2
STEPS = 7
LANES = 2 * BLOCK
CUTS = (0, 22, 41, 49)


def differs(a, b):
    return a + b - 2 * a * b


def kernel(
    amp, integ, out, rows_a, ints, sums, from_core, from_x, late_in, from_all, from_last, to_y, from_y,
    total, to_mirror, from_mirror, to_late, from_late, direct_half, turned, upright,
    local_sem, iy_s, iy_r, ay_s, ay_r, al_s, al_r, up_s, up_r, dn_s, dn_r, c_s, c_r, x_s, x_r, lc_s, lc_r, all_s, all_r, last_s, last_r,
    y_s, y_r, m_s, m_r, lm_s, lm_r, d_s, d_r,
):
    row, col = lax.axis_index("row"), lax.axis_index("col")
    y, z = row // RING, row % RING
    hx, zx, yh, core = col // 8, (col // 4) % 2, (col // 2) % 2, col % 2
    half = integ.shape[1] // 2
    mine = pl.ds(pl.multiple_of(y * half, 128), half)
    theirs = pl.ds(pl.multiple_of((1 - y) * half, 128), half)
    cuts = [(128 * a, 128 * (b - a)) for a, b in zip(CUTS[:-1], CUTS[1:])]

    def dev(y_=y, z_=z, hx_=hx, zx_=zx, yh_=yh, core_=core):
        return (y_ * RING + z_, hx_ * 8 + zx_ * 4 + yh_ * 2 + core_)

    def group(distance):
        return (z + distance + RING) % RING

    def slot(d):
        return (d % 2) * 4 + d // 2

    def remote(src, dst, send, recv, device):
        return pltpu.make_async_remote_copy(
            src_ref=src, dst_ref=dst, send_sem=send, recv_sem=recv, device_id=device, device_id_type=MESH
        )

    barrier = pltpu.get_barrier_semaphore()

    def greet(device):
        pl.semaphore_signal(barrier, inc=1, device_id=device, device_id_type=MESH)

    near = [dev(z_=group(1)), dev(z_=group(-1)), dev(core_=1 - core)]
    for device in near:
        greet(device)

    def is_me(h, y_, z_):
        return jnp.logical_and(jnp.logical_and(h == hx, y_ == y), z_ == z)

    def greet_source(t, _):
        greet(((1 - y) * RING + z, 2 * t + core))

        @pl.when(2 * t + core != col)
        def _():
            greet((row, 2 * t + core))

        for y_ in range(2):

            @pl.when(jnp.logical_not(is_me(y, y_, t)))
            def _(y_=y_):
                greet(dev(hx_=y, y_=y_, z_=t))

        return 0

    lax.fori_loop(0, RING, greet_source, 0)
    pl.semaphore_wait(barrier, len(near) + 4 * RING - 1 - (1 - differs(hx, y)))

    upright[pl.ds(OCC * NOCC, 4 * LANES - OCC * NOCC), :] = jnp.zeros((4 * LANES - OCC * NOCC, LANES), jnp.float32)

    def cut_along_q(m):
        return m >= STEPS - 2

    def pieces(m):
        return range(len(cuts) if cut_along_q(m) else SUB)

    def block_at(distance, owner_y, m, u):
        if cut_along_q(m):
            start, size, columns = 0, BLOCK, pl.ds(*cuts[u])
        else:
            start, size, columns = u * (BLOCK // SUB), BLOCK // SUB, pl.ds(0, half)
        start = pl.multiple_of(owner_y * BLOCK + start, BLOCK // SUB)
        return ints.at[slot(distance % RING), pl.ds(start, size), columns]

    def sub(u):
        return pl.ds(u * (BLOCK // SUB), BLOCK // SUB)

    def up_block(m):
        return -(m // 2), y if m % 2 == 0 else 1 - y

    def down_block(m):
        return (0, 0, 1, 1, 2, 2, 3)[m], (y, 1 - y, y, 1 - y, 1 - y, y, 1 - y)[m]

    def up(m, u):
        distance, owner = up_block(m)
        src = integ.at[sub(u), mine] if m == 0 else block_at(distance, owner, m, u)
        return remote(src, block_at(distance - 1, owner, m, u), up_s.at[m, u], up_r.at[m, u], dev(z_=group(1)))

    def down(m, u):
        distance, owner = down_block(m)
        src = integ.at[sub(u), mine] if m == 0 else block_at(distance, owner, m, u)
        return remote(src, block_at(distance + 1, owner, m, u), dn_s.at[m, u], dn_r.at[m, u], dev(z_=group(-1)))

    def up_arrives(n, u):
        distance, owner = up_block(n)
        place = block_at(distance - 1, owner, n, u)
        remote(place, place, up_s.at[n, u], up_r.at[n, u], dev(z_=group(1))).wait_recv()

    def down_arrives(n, u):
        distance, owner = down_block(n)
        place = block_at(distance + 1, owner, n, u)
        remote(place, place, dn_s.at[n, u], dn_r.at[n, u], dev(z_=group(-1))).wait_recv()

    def swap_i(u):
        return remote(integ.at[sub(u), theirs], block_at(0, y, 0, u), iy_s.at[u], iy_r.at[u], dev(y_=1 - y))

    def swap_i_arrives(u):
        place = block_at(0, 1 - y, 0, u)
        remote(place, place, iy_s.at[u], iy_r.at[u], dev(y_=1 - y)).wait_recv()

    def swap_a(i):
        src, dst = amp.at[pl.ds(i * NOCC, NOCC), theirs], rows_a.at[pl.ds((OCC + i) * NOCC, NOCC)]
        return remote(src, dst, ay_s.at[i], ay_r.at[i], dev(y_=1 - y))

    def swap_cut(i, k):
        start, width = cuts[k]
        src = amp.at[pl.ds(i * NOCC, NOCC), pl.ds(pl.multiple_of((1 - y) * half + start, 128), width)]
        dst = rows_a.at[pl.ds((OCC + i) * NOCC, NOCC), pl.ds(start, width)]
        return remote(src, dst, al_s.at[i - OCC + 2, k], al_r.at[i - OCC + 2, k], dev(y_=1 - y))

    for u in range(SUB):
        swap_i(u).start()
        up(0, u).start()
        down(0, u).start()
    own_rows = pl.ds(pl.multiple_of(y * BLOCK, BLOCK), BLOCK)
    load_i = pltpu.make_async_copy(integ.at[:, mine], ints.at[slot(0), own_rows], local_sem.at[0])
    load_a = pltpu.make_async_copy(amp.at[:, mine], rows_a.at[pl.ds(0, OCC * NOCC)], local_sem.at[1])
    load_i.start()
    load_a.start()
    for u in range(SUB):
        swap_i_arrives(u)
        up(1, u).start()
        down(1, u).start()
        if u == 0:
            swap_a(0).start()
    swap_a(1).start()
    load_i.wait()
    load_a.wait()

    def product(first, count, at, blocks, k=None):
        columns, width = (pl.ds(0, half), half) if k is None else (pl.ds(*cuts[k]), cuts[k][1])
        value = lax.dot_general(
            rows_a[pl.ds(first * NOCC, count * NOCC), columns],
            ints[pl.ds(at, blocks), :, columns].reshape(blocks * LANES, width),
            NT,
            preferred_element_type=jnp.float32,
        )
        for q in range(blocks):
            part = value[:, q * LANES : (q + 1) * LANES].reshape(count, NOCC, LANES)
            if k is None or k == 0:
                sums[at + q, pl.ds(first, count)] = part
            else:
                sums[at + q, pl.ds(first, count)] += part

    def five_blocks(first, k=None):
        product(first, 1, slot(0), 2, k)
        product(first, 1, slot(6), 2, k)
        product(first, 1, slot(7), 1, k)

    def part_of(role):
        return (pl.ds(0, OCC), pl.ds(OCC, OCC - 2), pl.ds(2 * OCC - 2, 1), pl.ds(0, 2 * OCC - 1))[role]

    def is_kept(d):
        return group(d) % 2 == core

    def to_core(d, role):
        at = part_of(role)
        return remote(
            sums.at[slot(d), at], from_core.at[d // 2, at], c_s.at[d // 2, role % 3], c_r.at[d // 2, role % 3], dev(core_=1 - core)
        )

    def to_x(d, role, h, act):
        at, g = part_of(role), group(d)
        z2, z1 = g // 4, (g // 2) % 2
        delta = 2 * differs(h, hx) + differs(z2, zx)

        @pl.when(delta > 0)
        def _():
            act(
                remote(
                    sums.at[slot(d), at, pl.ds(h * HALF_J, HALF_J)], from_x.at[delta - 1, z1, at],
                    x_s.at[d // 2, role % 3, h], x_r.at[delta - 1, z1], dev(hx_=h, zx_=z2),
                )
            )

    def reduce_core(d, role):
        @pl.when(jnp.logical_not(is_kept(d)))
        def _():
            to_core(d, role).start()

    def reduce_x(d, role):
        @pl.when(is_kept(d))
        def _():
            to_core(d, role).wait_recv()
            at = part_of(role)
            sums[slot(d), at] += from_core[d // 2, at]
            for h in range(2):
                to_x(d, role, h, lambda copy: copy.start())

    def over_five(act):
        lax.fori_loop(0, 5, lambda t, _: (act(t + 3 * (t // 3)), 0)[1], 0)

    last = group(4)
    j_mine = pl.ds(pl.multiple_of(hx * HALF_J, 8), HALF_J)
    j_theirs = pl.ds(pl.multiple_of((1 - hx) * HALF_J, 8), HALF_J)
    most = pl.ds(0, OCC - 1)

    def unit(z1):
        return zx * 4 + z1 * 2 + core

    def kept_of(far):
        return most if far else pl.ds(0, OCC)

    def x_arrives(z1):
        for delta in range(3):
            place = from_x.at[delta, z1]
            remote(place, place, x_s.at[0, 0, 0], x_r.at[delta, z1], dev(hx_=1 - hx)).wait_recv()

    def x_sum(z1, far):
        at = pl.ds(OCC, OCC - 1) if far else pl.ds(0, OCC)
        value = sums[slot((unit(z1) - z + RING) % RING), at, j_mine, :]
        for delta in range(3):
            value = value + from_x[delta, z1, at]
        return value

    def y_copy(e):
        at = kept_of(e & 1)
        target = dev(yh_=1 - yh if e & 2 else yh, y_=1 - y if e & 1 else y)
        return remote(to_y.at[e - 1, at], from_y.at[e - 1, at], y_s.at[e - 1], y_r.at[e - 1], target)

    def y_send(e):
        to_y[e - 1, kept_of(e & 1)] = x_sum(1 - yh if e & 2 else yh, e & 1)
        y_copy(e).start()

    def y_stage():
        @pl.when(unit(1 - yh) != last)
        def _():
            x_arrives(1 - yh)
            y_send(2)
            y_send(3)

        @pl.when(unit(yh) != last)
        def _():
            x_arrives(yh)
            y_send(1)
            total[...] = x_sum(yh, 0)

    def y_sent():
        @pl.when(unit(1 - yh) != last)
        def _():
            y_copy(2).wait_send()
            y_copy(3).wait_send()

        @pl.when(unit(yh) != last)
        def _():
            y_copy(1).wait_send()

    def to_last(h, far):
        at = pl.ds(OCC, OCC - 1) if far else pl.ds(0, OCC)
        sender = y * RING + col // 2
        z2, z1 = last // 4, (last // 2) % 2
        target = dev(y_=1 - y if far else y, hx_=h, zx_=z2, yh_=z1)
        return remote(
            sums.at[slot(4), at, pl.ds(h * HALF_J, HALF_J)], from_last.at[sender, kept_of(far)],
            last_s.at[h, far], last_r.at[sender], target,
        )

    def each_last(act):
        for far in (1, 0):
            for h in range(2):
                if far:
                    act(to_last(h, far))
                else:

                    @pl.when(jnp.logical_not(jnp.logical_and(unit(yh) == last, h == hx)))
                    def _(h=h, far=far):
                        act(to_last(h, far))

    def reduce_last():
        @pl.when(is_kept(4))
        def _():
            to_core(4, 3).wait_recv()
            at = part_of(3)
            sums[slot(4), at] += from_core[2, at]
            each_last(lambda copy: copy.start())

    def last_sums():
        value = sums[slot(4), pl.ds(0, OCC), j_mine, :]
        total[...] = value

        def add(t, _):
            @pl.when(2 * t + core != col)
            def _():
                place = from_last.at[y * RING + t]
                remote(place, place, last_s.at[0, 0], last_r.at[y * RING + t], dev(hx_=1 - hx)).wait_recv()
                total[...] += from_last[y * RING + t]

            there = (1 - y) * RING + t
            place = from_last.at[there, most]
            remote(place, place, last_s.at[0, 0], last_r.at[there], dev(hx_=1 - hx)).wait_recv()
            total[most] += from_last[there, most]
            return 0

        lax.fori_loop(0, RING, add, 0)

    mirror = dev(hx_=1 - hx)

    def direct(k):
        at = pl.ds(OCC - 1, 1) if k else most
        return remote(total.at[at], direct_half.at[at], d_s.at[k], d_r.at[k], mirror)

    def mirror_copy(k, t, h):
        src, dst, send, recv = ((to_mirror, from_mirror, m_s, m_r), (to_late, from_late, lm_s, lm_r))[k]
        return remote(src.at[t], dst.at[row], send.at[t, h], recv.at[row], dev(hx_=h, y_=hx, z_=t))

    def each_mirror(act):
        def body(t, _):
            for h in range(2):

                @pl.when(jnp.logical_not(is_me(h, hx, t)))
                def _():
                    act(t, h)

            return 0

        lax.fori_loop(0, RING, body, 0)

    def mirror_arrives(k):
        dst, send, recv = ((from_mirror, m_s, m_r), (from_late, lm_s, lm_r))[k]

        def body(r, _):
            @pl.when(jnp.logical_not(is_me(y, r // RING, r % RING)))
            def _():
                place = dst.at[r]
                remote(place, place, send.at[0, 0], recv.at[r], mirror).wait_recv()

            return 0

        lax.fori_loop(0, 2 * RING, body, 0)

    def spread():
        direct(0).start()
        for t in range(RING):
            for b in range(OCC):
                to_mirror[t, pl.ds(b * 4, 4), :] = total[most, t * OCC + b, :]
        each_mirror(lambda t, h: mirror_copy(0, t, h).start())

        @pl.when(hx == y)
        def _():
            from_mirror[row] = to_mirror[z]

    kept = (z + core) % 2
    late_core = remote(
        sums.at[pl.ds(4 * (1 - kept), 4), 2 * OCC - 1], late_in, lc_s, lc_r, dev(core_=1 - core)
    )

    def to_owner(q, h):
        d = 2 * q + kept
        src = sums.at[slot(d), 2 * OCC - 1, pl.ds(h * HALF_J, HALF_J)]
        owner = h * RING + group(d)
        return remote(src, from_all.at[col // 2], all_s.at[q, h], all_r.at[col // 2], ((1 - y) * RING + z, owner))

    def each_owner(act):
        def body(q, _):
            for h in range(2):
                act(to_owner(q, h))
            return 0

        lax.fori_loop(0, RING // 2, body, 0)

    product(0, OCC, slot(0), 1)
    reduce_core(0, 0)
    for n in range(STEPS - 2):
        if n == 4:
            for k in pieces(5):
                down(5, k).start()
        for u in pieces(n):
            up_arrives(n, u)
            if n + 2 < STEPS - 2:
                up(n + 2, u).start()
            down_arrives(n, u)
            if n in (0, 1):
                down(n + 2, u).start()
            elif n == 3:
                down(4, u).start()
        if n == 3:
            for k in pieces(5):
                up(5, k).start()
        elif n == 4:
            for k in pieces(6):
                up(6, k).start()
                down(6, k).start()
        if n == 1:
            swap_a(2).start()
        elif n in (2, 3):
            for k in range(len(cuts)):
                swap_cut(n + 1, k).start()
        if n == 0:
            reduce_x(0, 0)
        elif n in (1, 3):
            d = (n + 1) // 2
            for distance in (d, RING - d):
                product(0, OCC + d - 1, slot(distance), 1)
                reduce_core(distance, 0)
            for distance in (d, RING - d):
                reduce_x(distance, 0)
        if n == 2:
            swap_a(0).wait_recv()
            for distance in (0, 1, 7):
                product(OCC, 1, slot(distance), 1)
        elif n == 3:
            swap_a(1).wait_recv()
            five_blocks(OCC + 1)
        elif n == 4:
            swap_a(2).wait_recv()
            five_blocks(OCC + 2)
            over_five(lambda d: reduce_core(d, 1))
            over_five(lambda d: reduce_x(d, 1))

    def ring_sent(steps):
        for m in steps:
            for u in pieces(m):
                up(m, u).wait_send()
                down(m, u).wait_send()

    def sums_sent(d, role):
        @pl.when(jnp.logical_not(is_kept(d)))
        def _():
            to_core(d, role).wait_send()

        @pl.when(is_kept(d))
        def _():
            if isinstance(d, int) and d == 4:
                each_last(lambda copy: copy.wait_send())
            else:
                for h in range(2):
                    to_x(d, role, h, lambda copy: copy.wait_send())

    for u in range(SUB):
        swap_i(u).wait_send()
    ring_sent(range(4))
    for i in range(2):
        swap_a(i).wait_send()

    for k in range(len(cuts)):
        up_arrives(5, k)
        down_arrives(5, k)
        swap_cut(3, k).wait_recv()
        product(0, 2 * OCC - 1, slot(3), 2, k)
        five_blocks(2 * OCC - 2, k)
    for d in (3, 5):
        reduce_core(d, 3)
    over_five(lambda d: reduce_core(d, 2))
    for d in (3, 5):
        reduce_x(d, 3)
    over_five(lambda d: reduce_x(d, 2))

    ring_sent((4,))
    swap_a(2).wait_send()
    for role in range(2):
        over_five(lambda d, role=role: sums_sent(d, role))

    final = len(cuts) - 1
    for k in range(len(cuts)):
        up_arrives(6, k)
        down_arrives(6, k)
        product(0, 2 * OCC - 1, slot(4), 1, k)
        if k == 0:
            y_stage()
        if k == final:
            reduce_core(4, 3)
        for late in {0: (0,), final: range(1, final)}.get(k, ()):
            swap_cut(4, late).wait_recv()
            product(2 * OCC - 1, 1, 0, 4, late)
            product(2 * OCC - 1, 1, 4, 4, late)
    reduce_last()
    swap_cut(4, final).wait_recv()
    product(2 * OCC - 1, 1, 4 * (1 - kept), 4, final)
    late_core.start()
    product(2 * OCC - 1, 1, 4 * kept, 4, final)
    late_core.wait_recv()
    sums[pl.ds(4 * kept, 4), 2 * OCC - 1] += late_in[...]
    each_owner(lambda copy: copy.start())

    @pl.when(unit(yh) != last)
    def _():
        for e in (2, 3, 1):
            y_copy(e).wait_recv()
        total[...] += from_y[1]
        total[most] += from_y[0, most] + from_y[2, most]
        spread()

    @pl.when(unit(yh) == last)
    def _():
        last_sums()
        spread()

    def late_arrives(r, _):
        place = from_all.at[r]
        remote(place, place, all_s.at[0, 0], all_r.at[r], mirror).wait_recv()
        return 0

    lax.fori_loop(0, RING, late_arrives, 0)
    value = total[OCC - 1]
    for r in range(RING):
        value = value + from_all[r]
    total[OCC - 1] = value
    for t in range(RING):
        to_late[t, pl.ds(0, OCC), :] = total[OCC - 1, pl.ds(t * OCC, OCC), :]
    each_mirror(lambda t, h: mirror_copy(1, t, h).start())
    direct(1).start()

    @pl.when(hx == y)
    def _():
        from_late[row] = to_late[z]

    ring_sent((5, 6))
    for k in range(len(cuts)):
        swap_cut(3, k).wait_send()
        swap_cut(4, k).wait_send()
    over_five(lambda d: sums_sent(d, 2))
    for d in (3, 4, 5):
        sums_sent(d, 3)

    late_core.wait_send()
    each_owner(lambda copy: copy.wait_send())
    y_sent()
    mirror_arrives(0)
    for r in range(2 * RING):
        for b in range(OCC):
            turned[b, pl.ds(r * OCC, OCC - 1), :] = from_mirror[r, pl.ds(b * 4, 4), :]
    direct(0).wait_recv()

    direct(0).wait_send()
    each_mirror(lambda t, h: mirror_copy(0, t, h).wait_send())
    mirror_arrives(1)
    for r in range(2 * RING):
        turned[:, r * OCC + OCC - 1, :] = from_late[r, pl.ds(0, OCC), :]
    direct(1).wait_recv()

    def finish(straight, swapped):
        straight, swapped = (v.reshape(OCC * HALF_J, LANES) for v in (straight, swapped))
        here = jnp.where(hx == 0, straight, swapped)
        there = jnp.where(hx == 0, swapped, straight)
        value = here + pltpu.roll(there, BLOCK, 1)
        return [value[i * HALF_J : (i + 1) * HALF_J] for i in range(OCC)]

    for h, straight in ((hx, total), (1 - hx, direct_half)):
        at = pl.ds(pl.multiple_of(h * HALF_J, 8), HALF_J)
        for i, value in enumerate(finish(straight[...], turned[:, at, :])):
            upright[pl.ds(pl.multiple_of(i * NOCC + h * HALF_J, 8), HALF_J), :] = value
    out[...] = upright[...].T[:BLOCK, : OCC * NOCC]

    direct(1).wait_send()
    each_mirror(lambda t, h: mirror_copy(1, t, h).wait_send())


def on_device(amplitudes, integrals, residual_in):
    pairs, depth = amplitudes.shape
    half = depth // 2
    bf16, f32 = jnp.bfloat16, jnp.float32
    dma = pltpu.SemaphoreType.DMA
    cuts = len(CUTS) - 1
    ladder = pl.pallas_call(
        kernel,
        out_shape=jax.ShapeDtypeStruct((BLOCK, pairs), f32),
        in_specs=[pl.BlockSpec(memory_space=pltpu.HBM)] * 2,
        out_specs=pl.BlockSpec(memory_space=pltpu.VMEM),
        scratch_shapes=[
            pltpu.VMEM((2 * pairs, half), bf16),
            pltpu.VMEM((RING, LANES, half), bf16),
            pltpu.VMEM((RING, 2 * OCC, NOCC, LANES), f32),
            pltpu.VMEM((RING // 2, 2 * OCC - 1, NOCC, LANES), f32),
            pltpu.VMEM((3, 2, 2 * OCC - 1, HALF_J, LANES), f32),
            pltpu.VMEM((RING // 2, NOCC, LANES), f32),
            pltpu.VMEM((RING, HALF_J, LANES), f32),
            pltpu.VMEM((2 * RING, OCC, HALF_J, LANES), f32),
            pltpu.VMEM((3, OCC, HALF_J, LANES), f32),
            pltpu.VMEM((3, OCC, HALF_J, LANES), f32),
            pltpu.VMEM((OCC, HALF_J, LANES), f32),
            pltpu.VMEM((RING, 24, LANES), f32),
            pltpu.VMEM((2 * RING, 24, LANES), f32),
            pltpu.VMEM((RING, 8, LANES), f32),
            pltpu.VMEM((2 * RING, 8, LANES), f32),
            pltpu.VMEM((OCC, HALF_J, LANES), f32),
            pltpu.VMEM((OCC, NOCC, LANES), f32),
            pltpu.VMEM((4 * LANES, LANES), f32),
            dma((2,)),
            dma((SUB,)),
            dma((SUB,)),
            dma((OCC - 2,)),
            dma((OCC - 2,)),
            dma((2, cuts)),
            dma((2, cuts)),
            dma((STEPS, cuts)),
            dma((STEPS, cuts)),
            dma((STEPS, cuts)),
            dma((STEPS, cuts)),
            dma((RING // 2, 3)),
            dma((RING // 2, 3)),
            dma((RING // 2, 3, 2)),
            dma((3, 2)),
            dma,
            dma,
            dma((RING // 2, 2)),
            dma((RING,)),
            dma((2, 2)),
            dma((2 * RING,)),
            dma((3,)),
            dma((3,)),
            dma((RING, 2)),
            dma((2 * RING,)),
            dma((RING, 2)),
            dma((2 * RING,)),
            dma((2,)),
            dma((2,)),
        ],
        compiler_params=pltpu.CompilerParams(
            collective_id=0, has_side_effects=True, vmem_limit_bytes=60 * 1024 * 1024
        ),
        cost_estimate=pl.CostEstimate(
            flops=2 * pairs * depth * 16 * BLOCK, bytes_accessed=4 * pairs * depth, transcendentals=0
        ),
        name="ladder",
    )(amplitudes, integrals)
    return residual_in + ladder


def solution(mesh):
    placed = (P("row", "col"), P("row", "col"), P("col", "row"))
    return jax.shard_map(
        on_device, mesh=mesh, in_specs=placed, out_specs=P("col", "row"), check_vma=False
    )
```

```python
import jax
import jax.numpy as jnp
from jax import lax
from jax.experimental import pallas as pl
from jax.experimental.pallas import tpu as pltpu
from jax.sharding import PartitionSpec as P

MESH = pl.DeviceIdType.MESH
NT = (((1,), (1,)), ((), ()))
RING = 8
BLOCK = 64
OCC = 5
NOCC = 80
HALF_J = 40
SUB = 2
STEPS = 7
LANES = 2 * BLOCK
CUTS = (0, 22, 41, 49)


def differs(a, b):
    return a + b - 2 * a * b


def kernel(
    amp, integ, out, rows_a, ints, sums, from_core, from_x, late_in, from_all, from_last, to_y, from_y,
    total, to_mirror, from_mirror, to_late, from_late, direct_half, turned, upright,
    local_sem, iy_s, iy_r, ay_s, ay_r, al_s, al_r, up_s, up_r, dn_s, dn_r, c_s, c_r, x_s, x_r, lc_s, lc_r, all_s, all_r, last_s, last_r,
    y_s, y_r, m_s, m_r, lm_s, lm_r, d_s, d_r,
):
    row, col = lax.axis_index("row"), lax.axis_index("col")
    y, z = row // RING, row % RING
    hx, zx, yh, core = col // 8, (col // 4) % 2, (col // 2) % 2, col % 2
    half = integ.shape[1] // 2
    mine = pl.ds(pl.multiple_of(y * half, 128), half)
    theirs = pl.ds(pl.multiple_of((1 - y) * half, 128), half)
    cuts = [(128 * a, 128 * (b - a)) for a, b in zip(CUTS[:-1], CUTS[1:])]

    def dev(y_=y, z_=z, hx_=hx, zx_=zx, yh_=yh, core_=core):
        return (y_ * RING + z_, hx_ * 8 + zx_ * 4 + yh_ * 2 + core_)

    def group(distance):
        return (z + distance + RING) % RING

    def slot(d):
        return (d % 2) * 4 + d // 2

    def remote(src, dst, send, recv, device):
        return pltpu.make_async_remote_copy(
            src_ref=src, dst_ref=dst, send_sem=send, recv_sem=recv, device_id=device, device_id_type=MESH
        )

    barrier = pltpu.get_barrier_semaphore()

    def greet(device):
        pl.semaphore_signal(barrier, inc=1, device_id=device, device_id_type=MESH)

    near = [dev(z_=group(1)), dev(z_=group(-1)), dev(core_=1 - core)]
    for device in near:
        greet(device)

    def is_me(h, y_, z_):
        return jnp.logical_and(jnp.logical_and(h == hx, y_ == y), z_ == z)

    def greet_source(t, _):
        greet(((1 - y) * RING + z, 2 * t + core))

        @pl.when(2 * t + core != col)
        def _():
            greet((row, 2 * t + core))

        for y_ in range(2):

            @pl.when(jnp.logical_not(is_me(y, y_, t)))
            def _(y_=y_):
                greet(dev(hx_=y, y_=y_, z_=t))

        return 0

    lax.fori_loop(0, RING, greet_source, 0)
    pl.semaphore_wait(barrier, len(near) + 4 * RING - 1 - (1 - differs(hx, y)))

    upright[pl.ds(OCC * NOCC, 4 * LANES - OCC * NOCC), :] = jnp.zeros((4 * LANES - OCC * NOCC, LANES), jnp.float32)

    def cut_along_q(m):
        return m >= STEPS - 2

    def pieces(m):
        return range(len(cuts) if cut_along_q(m) else SUB)

    def block_at(distance, owner_y, m, u):
        if cut_along_q(m):
            start, size, columns = 0, BLOCK, pl.ds(*cuts[u])
        else:
            start, size, columns = u * (BLOCK // SUB), BLOCK // SUB, pl.ds(0, half)
        start = pl.multiple_of(owner_y * BLOCK + start, BLOCK // SUB)
        return ints.at[slot(distance % RING), pl.ds(start, size), columns]

    def sub(u):
        return pl.ds(u * (BLOCK // SUB), BLOCK // SUB)

    def up_block(m):
        return -(m // 2), y if m % 2 == 0 else 1 - y

    def down_block(m):
        return (0, 0, 1, 1, 2, 2, 3)[m], (y, 1 - y, y, 1 - y, 1 - y, y, 1 - y)[m]

    def up(m, u):
        distance, owner = up_block(m)
        src = integ.at[sub(u), mine] if m == 0 else block_at(distance, owner, m, u)
        return remote(src, block_at(distance - 1, owner, m, u), up_s.at[m, u], up_r.at[m, u], dev(z_=group(1)))

    def down(m, u):
        distance, owner = down_block(m)
        src = integ.at[sub(u), mine] if m == 0 else block_at(distance, owner, m, u)
        return remote(src, block_at(distance + 1, owner, m, u), dn_s.at[m, u], dn_r.at[m, u], dev(z_=group(-1)))

    def up_arrives(n, u):
        distance, owner = up_block(n)
        place = block_at(distance - 1, owner, n, u)
        remote(place, place, up_s.at[n, u], up_r.at[n, u], dev(z_=group(1))).wait_recv()

    def down_arrives(n, u):
        distance, owner = down_block(n)
        place = block_at(distance + 1, owner, n, u)
        remote(place, place, dn_s.at[n, u], dn_r.at[n, u], dev(z_=group(-1))).wait_recv()

    def swap_i(u):
        return remote(integ.at[sub(u), theirs], block_at(0, y, 0, u), iy_s.at[u], iy_r.at[u], dev(y_=1 - y))

    def swap_i_arrives(u):
        place = block_at(0, 1 - y, 0, u)
        remote(place, place, iy_s.at[u], iy_r.at[u], dev(y_=1 - y)).wait_recv()

    def swap_a(i):
        src, dst = amp.at[pl.ds(i * NOCC, NOCC), theirs], rows_a.at[pl.ds((OCC + i) * NOCC, NOCC)]
        return remote(src, dst, ay_s.at[i], ay_r.at[i], dev(y_=1 - y))

    def swap_cut(i, k):
        start, width = cuts[k]
        src = amp.at[pl.ds(i * NOCC, NOCC), pl.ds(pl.multiple_of((1 - y) * half + start, 128), width)]
        dst = rows_a.at[pl.ds((OCC + i) * NOCC, NOCC), pl.ds(start, width)]
        return remote(src, dst, al_s.at[i - OCC + 2, k], al_r.at[i - OCC + 2, k], dev(y_=1 - y))

    for u in range(SUB):
        swap_i(u).start()
        up(0, u).start()
        down(0, u).start()
    own_rows = pl.ds(pl.multiple_of(y * BLOCK, BLOCK), BLOCK)
    load_i = pltpu.make_async_copy(integ.at[:, mine], ints.at[slot(0), own_rows], local_sem.at[0])
    load_a = pltpu.make_async_copy(amp.at[:, mine], rows_a.at[pl.ds(0, OCC * NOCC)], local_sem.at[1])
    load_i.start()
    load_a.start()
    for u in range(SUB):
        swap_i_arrives(u)
        up(1, u).start()
        down(1, u).start()
        if u == 0:
            swap_a(0).start()
    swap_a(1).start()
    load_i.wait()
    load_a.wait()

    def product(first, count, at, blocks, k=None):
        columns, width = (pl.ds(0, half), half) if k is None else (pl.ds(*cuts[k]), cuts[k][1])
        value = lax.dot_general(
            rows_a[pl.ds(first * NOCC, count * NOCC), columns],
            ints[pl.ds(at, blocks), :, columns].reshape(blocks * LANES, width),
            NT,
            preferred_element_type=jnp.float32,
        )
        for q in range(blocks):
            part = value[:, q * LANES : (q + 1) * LANES].reshape(count, NOCC, LANES)
            if k is None or k == 0:
                sums[at + q, pl.ds(first, count)] = part
            else:
                sums[at + q, pl.ds(first, count)] += part

    def five_blocks(first, k=None):
        product(first, 1, slot(0), 2, k)
        product(first, 1, slot(6), 2, k)
        product(first, 1, slot(7), 1, k)

    def part_of(role):
        return (pl.ds(0, OCC), pl.ds(OCC, OCC - 2), pl.ds(2 * OCC - 2, 1), pl.ds(0, 2 * OCC - 1))[role]

    def is_kept(d):
        return group(d) % 2 == core

    def to_core(d, role):
        at = part_of(role)
        return remote(
            sums.at[slot(d), at], from_core.at[d // 2, at], c_s.at[d // 2, role % 3], c_r.at[d // 2, role % 3], dev(core_=1 - core)
        )

    def to_x(d, role, h, act):
        at, g = part_of(role), group(d)
        z2, z1 = g // 4, (g // 2) % 2
        delta = 2 * differs(h, hx) + differs(z2, zx)

        @pl.when(delta > 0)
        def _():
            act(
                remote(
                    sums.at[slot(d), at, pl.ds(h * HALF_J, HALF_J)], from_x.at[delta - 1, z1, at],
                    x_s.at[d // 2, role % 3, h], x_r.at[delta - 1, z1], dev(hx_=h, zx_=z2),
                )
            )

    def reduce_core(d, role):
        @pl.when(jnp.logical_not(is_kept(d)))
        def _():
            to_core(d, role).start()

    def reduce_x(d, role):
        @pl.when(is_kept(d))
        def _():
            to_core(d, role).wait_recv()
            at = part_of(role)
            sums[slot(d), at] += from_core[d // 2, at]
            for h in range(2):
                to_x(d, role, h, lambda copy: copy.start())

    def over_five(act):
        lax.fori_loop(0, 5, lambda t, _: (act(t + 3 * (t // 3)), 0)[1], 0)

    last = group(4)
    j_mine = pl.ds(pl.multiple_of(hx * HALF_J, 8), HALF_J)
    j_theirs = pl.ds(pl.multiple_of((1 - hx) * HALF_J, 8), HALF_J)
    most = pl.ds(0, OCC - 1)

    def unit(z1):
        return zx * 4 + z1 * 2 + core

    def kept_of(far):
        return most if far else pl.ds(0, OCC)

    def x_arrives(z1):
        for delta in range(3):
            place = from_x.at[delta, z1]
            remote(place, place, x_s.at[0, 0, 0], x_r.at[delta, z1], dev(hx_=1 - hx)).wait_recv()

    def x_sum(z1, far):
        at = pl.ds(OCC, OCC - 1) if far else pl.ds(0, OCC)
        value = sums[slot((unit(z1) - z + RING) % RING), at, j_mine, :]
        for delta in range(3):
            value = value + from_x[delta, z1, at]
        return value

    def y_copy(e):
        at = kept_of(e & 1)
        target = dev(yh_=1 - yh if e & 2 else yh, y_=1 - y if e & 1 else y)
        return remote(to_y.at[e - 1, at], from_y.at[e - 1, at], y_s.at[e - 1], y_r.at[e - 1], target)

    def y_send(e):
        to_y[e - 1, kept_of(e & 1)] = x_sum(1 - yh if e & 2 else yh, e & 1)
        y_copy(e).start()

    def y_stage():
        @pl.when(unit(1 - yh) != last)
        def _():
            x_arrives(1 - yh)
            y_send(2)
            y_send(3)

        @pl.when(unit(yh) != last)
        def _():
            x_arrives(yh)
            y_send(1)
            total[...] = x_sum(yh, 0)

    def y_sent():
        @pl.when(unit(1 - yh) != last)
        def _():
            y_copy(2).wait_send()
            y_copy(3).wait_send()

        @pl.when(unit(yh) != last)
        def _():
            y_copy(1).wait_send()

    def to_last(h, far):
        at = pl.ds(OCC, OCC - 1) if far else pl.ds(0, OCC)
        sender = y * RING + col // 2
        z2, z1 = last // 4, (last // 2) % 2
        target = dev(y_=1 - y if far else y, hx_=h, zx_=z2, yh_=z1)
        return remote(
            sums.at[slot(4), at, pl.ds(h * HALF_J, HALF_J)], from_last.at[sender, kept_of(far)],
            last_s.at[h, far], last_r.at[sender], target,
        )

    def each_last(act):
        for far in (1, 0):
            for h in range(2):
                if far:
                    act(to_last(h, far))
                else:

                    @pl.when(jnp.logical_not(jnp.logical_and(unit(yh) == last, h == hx)))
                    def _(h=h, far=far):
                        act(to_last(h, far))

    def reduce_last():
        @pl.when(is_kept(4))
        def _():
            to_core(4, 3).wait_recv()
            at = part_of(3)
            sums[slot(4), at] += from_core[2, at]
            each_last(lambda copy: copy.start())

    def last_sums():
        value = sums[slot(4), pl.ds(0, OCC), j_mine, :]
        total[...] = value

        def add(t, _):
            @pl.when(2 * t + core != col)
            def _():
                place = from_last.at[y * RING + t]
                remote(place, place, last_s.at[0, 0], last_r.at[y * RING + t], dev(hx_=1 - hx)).wait_recv()
                total[...] += from_last[y * RING + t]

            there = (1 - y) * RING + t
            place = from_last.at[there, most]
            remote(place, place, last_s.at[0, 0], last_r.at[there], dev(hx_=1 - hx)).wait_recv()
            total[most] += from_last[there, most]
            return 0

        lax.fori_loop(0, RING, add, 0)

    mirror = dev(hx_=1 - hx)

    def direct(k):
        at = pl.ds(OCC - 1, 1) if k else most
        return remote(total.at[at], direct_half.at[at], d_s.at[k], d_r.at[k], mirror)

    def mirror_copy(k, t, h):
        src, dst, send, recv = ((to_mirror, from_mirror, m_s, m_r), (to_late, from_late, lm_s, lm_r))[k]
        return remote(src.at[t], dst.at[row], send.at[t, h], recv.at[row], dev(hx_=h, y_=hx, z_=t))

    def each_mirror(act):
        def body(t, _):
            for h in range(2):

                @pl.when(jnp.logical_not(is_me(h, hx, t)))
                def _():
                    act(t, h)

            return 0

        lax.fori_loop(0, RING, body, 0)

    def mirror_arrives(k):
        dst, send, recv = ((from_mirror, m_s, m_r), (from_late, lm_s, lm_r))[k]

        def body(r, _):
            @pl.when(jnp.logical_not(is_me(y, r // RING, r % RING)))
            def _():
                place = dst.at[r]
                remote(place, place, send.at[0, 0], recv.at[r], mirror).wait_recv()

            return 0

        lax.fori_loop(0, 2 * RING, body, 0)

    def spread():
        direct(0).start()
        for t in range(RING):
            for b in range(OCC):
                to_mirror[t, pl.ds(b * 4, 4), :] = total[most, t * OCC + b, :]
        each_mirror(lambda t, h: mirror_copy(0, t, h).start())

        @pl.when(hx == y)
        def _():
            from_mirror[row] = to_mirror[z]

    kept = (z + core) % 2
    late_core = remote(
        sums.at[pl.ds(4 * (1 - kept), 4), 2 * OCC - 1], late_in, lc_s, lc_r, dev(core_=1 - core)
    )

    def to_owner(q, h):
        d = 2 * q + kept
        src = sums.at[slot(d), 2 * OCC - 1, pl.ds(h * HALF_J, HALF_J)]
        owner = h * RING + group(d)
        return remote(src, from_all.at[col // 2], all_s.at[q, h], all_r.at[col // 2], ((1 - y) * RING + z, owner))

    def each_owner(act):
        def body(q, _):
            for h in range(2):
                act(to_owner(q, h))
            return 0

        lax.fori_loop(0, RING // 2, body, 0)

    product(0, OCC, slot(0), 1)
    reduce_core(0, 0)
    for n in range(STEPS - 2):
        if n == 4:
            for k in pieces(5):
                down(5, k).start()
        for u in pieces(n):
            up_arrives(n, u)
            if n + 2 < STEPS - 2:
                up(n + 2, u).start()
            down_arrives(n, u)
            if n in (0, 1):
                down(n + 2, u).start()
            elif n == 3:
                down(4, u).start()
        if n == 3:
            for k in pieces(5):
                up(5, k).start()
        elif n == 4:
            for k in pieces(6):
                up(6, k).start()
                down(6, k).start()
        if n == 1:
            swap_a(2).start()
        elif n in (2, 3):
            for k in range(len(cuts)):
                swap_cut(n + 1, k).start()
        if n == 0:
            reduce_x(0, 0)
        elif n in (1, 3):
            d = (n + 1) // 2
            for distance in (d, RING - d):
                product(0, OCC + d - 1, slot(distance), 1)
                reduce_core(distance, 0)
            for distance in (d, RING - d):
                reduce_x(distance, 0)
        if n == 2:
            swap_a(0).wait_recv()
            for distance in (0, 1, 7):
                product(OCC, 1, slot(distance), 1)
        elif n == 3:
            swap_a(1).wait_recv()
            five_blocks(OCC + 1)
        elif n == 4:
            swap_a(2).wait_recv()
            five_blocks(OCC + 2)
            over_five(lambda d: reduce_core(d, 1))
            over_five(lambda d: reduce_x(d, 1))

    def ring_sent(steps):
        for m in steps:
            for u in pieces(m):
                up(m, u).wait_send()
                down(m, u).wait_send()

    def sums_sent(d, role):
        @pl.when(jnp.logical_not(is_kept(d)))
        def _():
            to_core(d, role).wait_send()

        @pl.when(is_kept(d))
        def _():
            if isinstance(d, int) and d == 4:
                each_last(lambda copy: copy.wait_send())
            else:
                for h in range(2):
                    to_x(d, role, h, lambda copy: copy.wait_send())

    for u in range(SUB):
        swap_i(u).wait_send()
    ring_sent(range(4))
    for i in range(2):
        swap_a(i).wait_send()

    for k in range(len(cuts)):
        up_arrives(5, k)
        down_arrives(5, k)
        swap_cut(3, k).wait_recv()
        product(0, 2 * OCC - 1, slot(3), 2, k)
        five_blocks(2 * OCC - 2, k)
    for d in (3, 5):
        reduce_core(d, 3)
    over_five(lambda d: reduce_core(d, 2))
    for d in (3, 5):
        reduce_x(d, 3)
    over_five(lambda d: reduce_x(d, 2))

    ring_sent((4,))
    swap_a(2).wait_send()
    for role in range(2):
        over_five(lambda d, role=role: sums_sent(d, role))

    final = len(cuts) - 1
    for k in range(len(cuts)):
        up_arrives(6, k)
        down_arrives(6, k)
        product(0, 2 * OCC - 1, slot(4), 1, k)
        if k == 0:
            y_stage()
        if k == final:
            reduce_core(4, 3)
        for late in {0: (0,), final: range(1, final)}.get(k, ()):
            swap_cut(4, late).wait_recv()
            product(2 * OCC - 1, 1, 0, 4, late)
            product(2 * OCC - 1, 1, 4, 4, late)
    reduce_last()
    swap_cut(4, final).wait_recv()
    product(2 * OCC - 1, 1, 4 * (1 - kept), 4, final)
    late_core.start()
    product(2 * OCC - 1, 1, 4 * kept, 4, final)
    late_core.wait_recv()
    sums[pl.ds(4 * kept, 4), 2 * OCC - 1] += late_in[...]
    each_owner(lambda copy: copy.start())

    @pl.when(unit(yh) != last)
    def _():
        for e in (2, 3, 1):
            y_copy(e).wait_recv()
        total[...] += from_y[1]
        total[most] += from_y[0, most] + from_y[2, most]
        spread()

    @pl.when(unit(yh) == last)
    def _():
        last_sums()
        spread()

    def late_arrives(r, _):
        place = from_all.at[r]
        remote(place, place, all_s.at[0, 0], all_r.at[r], mirror).wait_recv()
        return 0

    lax.fori_loop(0, RING, late_arrives, 0)
    value = total[OCC - 1]
    for r in range(RING):
        value = value + from_all[r]
    total[OCC - 1] = value
    for t in range(RING):
        to_late[t, pl.ds(0, OCC), :] = total[OCC - 1, pl.ds(t * OCC, OCC), :]
    each_mirror(lambda t, h: mirror_copy(1, t, h).start())
    direct(1).start()

    @pl.when(hx == y)
    def _():
        from_late[row] = to_late[z]

    ring_sent((5, 6))
    for k in range(len(cuts)):
        swap_cut(3, k).wait_send()
        swap_cut(4, k).wait_send()
    over_five(lambda d: sums_sent(d, 2))
    for d in (3, 4, 5):
        sums_sent(d, 3)

    late_core.wait_send()
    each_owner(lambda copy: copy.wait_send())
    y_sent()
    mirror_arrives(0)
    for r in range(2 * RING):
        for b in range(OCC):
            turned[b, pl.ds(r * OCC, OCC - 1), :] = from_mirror[r, pl.ds(b * 4, 4), :]
    direct(0).wait_recv()

    direct(0).wait_send()
    each_mirror(lambda t, h: mirror_copy(0, t, h).wait_send())
    direct(1).wait_send()
    each_mirror(lambda t, h: mirror_copy(1, t, h).wait_send())
    mirror_arrives(1)
    for r in range(2 * RING):
        turned[:, r * OCC + OCC - 1, :] = from_late[r, pl.ds(0, OCC), :]
    direct(1).wait_recv()

    def finish(straight, swapped):
        straight, swapped = (v.reshape(OCC * HALF_J, LANES) for v in (straight, swapped))
        here = jnp.where(hx == 0, straight, swapped)
        there = jnp.where(hx == 0, swapped, straight)
        value = here + pltpu.roll(there, BLOCK, 1)
        return [value[i * HALF_J : (i + 1) * HALF_J] for i in range(OCC)]

    for h, straight in ((hx, total), (1 - hx, direct_half)):
        at = pl.ds(pl.multiple_of(h * HALF_J, 8), HALF_J)
        for i, value in enumerate(finish(straight[...], turned[:, at, :])):
            upright[pl.ds(pl.multiple_of(i * NOCC + h * HALF_J, 8), HALF_J), :] = value
    out[...] = upright[...].T[:BLOCK, : OCC * NOCC]


def on_device(amplitudes, integrals, residual_in):
    pairs, depth = amplitudes.shape
    half = depth // 2
    bf16, f32 = jnp.bfloat16, jnp.float32
    dma = pltpu.SemaphoreType.DMA
    cuts = len(CUTS) - 1
    ladder = pl.pallas_call(
        kernel,
        out_shape=jax.ShapeDtypeStruct((BLOCK, pairs), f32),
        in_specs=[pl.BlockSpec(memory_space=pltpu.HBM)] * 2,
        out_specs=pl.BlockSpec(memory_space=pltpu.VMEM),
        scratch_shapes=[
            pltpu.VMEM((2 * pairs, half), bf16),
            pltpu.VMEM((RING, LANES, half), bf16),
            pltpu.VMEM((RING, 2 * OCC, NOCC, LANES), f32),
            pltpu.VMEM((RING // 2, 2 * OCC - 1, NOCC, LANES), f32),
            pltpu.VMEM((3, 2, 2 * OCC - 1, HALF_J, LANES), f32),
            pltpu.VMEM((RING // 2, NOCC, LANES), f32),
            pltpu.VMEM((RING, HALF_J, LANES), f32),
            pltpu.VMEM((2 * RING, OCC, HALF_J, LANES), f32),
            pltpu.VMEM((3, OCC, HALF_J, LANES), f32),
            pltpu.VMEM((3, OCC, HALF_J, LANES), f32),
            pltpu.VMEM((OCC, HALF_J, LANES), f32),
            pltpu.VMEM((RING, 24, LANES), f32),
            pltpu.VMEM((2 * RING, 24, LANES), f32),
            pltpu.VMEM((RING, 8, LANES), f32),
            pltpu.VMEM((2 * RING, 8, LANES), f32),
            pltpu.VMEM((OCC, HALF_J, LANES), f32),
            pltpu.VMEM((OCC, NOCC, LANES), f32),
            pltpu.VMEM((4 * LANES, LANES), f32),
            dma((2,)),
            dma((SUB,)),
            dma((SUB,)),
            dma((OCC - 2,)),
            dma((OCC - 2,)),
            dma((2, cuts)),
            dma((2, cuts)),
            dma((STEPS, cuts)),
            dma((STEPS, cuts)),
            dma((STEPS, cuts)),
            dma((STEPS, cuts)),
            dma((RING // 2, 3)),
            dma((RING // 2, 3)),
            dma((RING // 2, 3, 2)),
            dma((3, 2)),
            dma,
            dma,
            dma((RING // 2, 2)),
            dma((RING,)),
            dma((2, 2)),
            dma((2 * RING,)),
            dma((3,)),
            dma((3,)),
            dma((RING, 2)),
            dma((2 * RING,)),
            dma((RING, 2)),
            dma((2 * RING,)),
            dma((2,)),
            dma((2,)),
        ],
        compiler_params=pltpu.CompilerParams(
            collective_id=0, has_side_effects=True, vmem_limit_bytes=53 * 1024 * 1024
        ),
        cost_estimate=pl.CostEstimate(
            flops=2 * pairs * depth * 16 * BLOCK, bytes_accessed=4 * pairs * depth, transcendentals=0
        ),
        name="ladder",
    )(amplitudes, integrals)
    return residual_in + ladder


def solution(mesh):
    placed = (P("row", "col"), P("row", "col"), P("col", "row"))
    return jax.shard_map(
        on_device, mesh=mesh, in_specs=placed, out_specs=P("col", "row"), check_vma=False
    )
```

```python
import jax
import jax.numpy as jnp
from jax import lax
from jax.experimental import pallas as pl
from jax.experimental.pallas import tpu as pltpu
from jax.sharding import PartitionSpec as P

MESH = pl.DeviceIdType.MESH
NT = (((1,), (1,)), ((), ()))
RING = 8
BLOCK = 64
OCC = 5
NOCC = 80
HALF_J = 40
SUB = 2
STEPS = 7
LANES = 2 * BLOCK
CUTS = (0, 22, 41, 49)


def differs(a, b):
    return a + b - 2 * a * b


def kernel(
    amp, integ, out, rows_a, ints, sums, from_core, from_x, late_in, from_all, from_last, to_y, from_y,
    total, to_mirror, from_mirror, to_late, from_late, direct_half, turned, upright,
    local_sem, iy_s, iy_r, ay_s, ay_r, al_s, al_r, up_s, up_r, dn_s, dn_r, c_s, c_r, x_s, x_r, lc_s, lc_r, all_s, all_r, last_s, last_r,
    y_s, y_r, m_s, m_r, lm_s, lm_r, d_s, d_r,
):
    row, col = lax.axis_index("row"), lax.axis_index("col")
    y, z = row // RING, row % RING
    hx, zx, yh, core = col // 8, (col // 4) % 2, (col // 2) % 2, col % 2
    half = integ.shape[1] // 2
    mine = pl.ds(pl.multiple_of(y * half, 128), half)
    theirs = pl.ds(pl.multiple_of((1 - y) * half, 128), half)
    cuts = [(128 * a, 128 * (b - a)) for a, b in zip(CUTS[:-1], CUTS[1:])]

    def dev(y_=y, z_=z, hx_=hx, zx_=zx, yh_=yh, core_=core):
        return (y_ * RING + z_, hx_ * 8 + zx_ * 4 + yh_ * 2 + core_)

    def group(distance):
        return (z + distance + RING) % RING

    def slot(d):
        return (d % 2) * 4 + d // 2

    def remote(src, dst, send, recv, device):
        return pltpu.make_async_remote_copy(
            src_ref=src, dst_ref=dst, send_sem=send, recv_sem=recv, device_id=device, device_id_type=MESH
        )

    barrier = pltpu.get_barrier_semaphore()

    def greet(device):
        pl.semaphore_signal(barrier, inc=1, device_id=device, device_id_type=MESH)

    near = [dev(z_=group(1)), dev(z_=group(-1)), dev(core_=1 - core)]
    for device in near:
        greet(device)

    def is_me(h, y_, z_):
        return jnp.logical_and(jnp.logical_and(h == hx, y_ == y), z_ == z)

    def greet_source(t, _):
        greet(((1 - y) * RING + z, 2 * t + core))

        @pl.when(2 * t + core != col)
        def _():
            greet((row, 2 * t + core))

        for y_ in range(2):

            @pl.when(jnp.logical_not(is_me(y, y_, t)))
            def _(y_=y_):
                greet(dev(hx_=y, y_=y_, z_=t))

        return 0

    lax.fori_loop(0, RING, greet_source, 0)
    pl.semaphore_wait(barrier, len(near) + 4 * RING - 1 - (1 - differs(hx, y)))

    upright[pl.ds(OCC * NOCC, 4 * LANES - OCC * NOCC), :] = jnp.zeros((4 * LANES - OCC * NOCC, LANES), jnp.float32)

    def cut_along_q(m):
        return m >= STEPS - 2

    def pieces(m):
        return range(len(cuts) if cut_along_q(m) else SUB)

    def block_at(distance, owner_y, m, u):
        if cut_along_q(m):
            start, size, columns = 0, BLOCK, pl.ds(*cuts[u])
        else:
            start, size, columns = u * (BLOCK // SUB), BLOCK // SUB, pl.ds(0, half)
        start = pl.multiple_of(owner_y * BLOCK + start, BLOCK // SUB)
        return ints.at[slot(distance % RING), pl.ds(start, size), columns]

    def sub(u):
        return pl.ds(u * (BLOCK // SUB), BLOCK // SUB)

    def up_block(m):
        return -(m // 2), y if m % 2 == 0 else 1 - y

    def down_block(m):
        return (0, 0, 1, 1, 2, 2, 3)[m], (y, 1 - y, y, 1 - y, 1 - y, y, 1 - y)[m]

    def up(m, u):
        distance, owner = up_block(m)
        src = integ.at[sub(u), mine] if m == 0 else block_at(distance, owner, m, u)
        return remote(src, block_at(distance - 1, owner, m, u), up_s.at[m, u], up_r.at[m, u], dev(z_=group(1)))

    def down(m, u):
        distance, owner = down_block(m)
        src = integ.at[sub(u), mine] if m == 0 else block_at(distance, owner, m, u)
        return remote(src, block_at(distance + 1, owner, m, u), dn_s.at[m, u], dn_r.at[m, u], dev(z_=group(-1)))

    def up_arrives(n, u):
        distance, owner = up_block(n)
        place = block_at(distance - 1, owner, n, u)
        remote(place, place, up_s.at[n, u], up_r.at[n, u], dev(z_=group(1))).wait_recv()

    def down_arrives(n, u):
        distance, owner = down_block(n)
        place = block_at(distance + 1, owner, n, u)
        remote(place, place, dn_s.at[n, u], dn_r.at[n, u], dev(z_=group(-1))).wait_recv()

    def swap_i(u):
        return remote(integ.at[sub(u), theirs], block_at(0, y, 0, u), iy_s.at[u], iy_r.at[u], dev(y_=1 - y))

    def swap_i_arrives(u):
        place = block_at(0, 1 - y, 0, u)
        remote(place, place, iy_s.at[u], iy_r.at[u], dev(y_=1 - y)).wait_recv()

    def swap_a(i):
        src, dst = amp.at[pl.ds(i * NOCC, NOCC), theirs], rows_a.at[pl.ds((OCC + i) * NOCC, NOCC)]
        return remote(src, dst, ay_s.at[i], ay_r.at[i], dev(y_=1 - y))

    def swap_cut(i, k):
        start, width = cuts[k]
        src = amp.at[pl.ds(i * NOCC, NOCC), pl.ds(pl.multiple_of((1 - y) * half + start, 128), width)]
        dst = rows_a.at[pl.ds((OCC + i) * NOCC, NOCC), pl.ds(start, width)]
        return remote(src, dst, al_s.at[i - OCC + 2, k], al_r.at[i - OCC + 2, k], dev(y_=1 - y))

    for u in range(SUB):
        swap_i(u).start()
        up(0, u).start()
        down(0, u).start()
    own_rows = pl.ds(pl.multiple_of(y * BLOCK, BLOCK), BLOCK)
    load_i = pltpu.make_async_copy(integ.at[:, mine], ints.at[slot(0), own_rows], local_sem.at[0])
    load_a = pltpu.make_async_copy(amp.at[:, mine], rows_a.at[pl.ds(0, OCC * NOCC)], local_sem.at[1])
    load_i.start()
    load_a.start()
    for u in range(SUB):
        swap_i_arrives(u)
        up(1, u).start()
        down(1, u).start()
        if u == 0:
            swap_a(0).start()
    swap_a(1).start()
    load_i.wait()
    load_a.wait()

    def product(first, count, at, blocks, k=None):
        columns, width = (pl.ds(0, half), half) if k is None else (pl.ds(*cuts[k]), cuts[k][1])
        value = lax.dot_general(
            rows_a[pl.ds(first * NOCC, count * NOCC), columns],
            ints[pl.ds(at, blocks), :, columns].reshape(blocks * LANES, width),
            NT,
            preferred_element_type=jnp.float32,
        )
        for q in range(blocks):
            part = value[:, q * LANES : (q + 1) * LANES].reshape(count, NOCC, LANES)
            if k is None or k == 0:
                sums[at + q, pl.ds(first, count)] = part
            else:
                sums[at + q, pl.ds(first, count)] += part

    def five_blocks(first, k=None):
        product(first, 1, slot(0), 2, k)
        product(first, 1, slot(6), 2, k)
        product(first, 1, slot(7), 1, k)

    def part_of(role):
        return (pl.ds(0, OCC), pl.ds(OCC, OCC - 2), pl.ds(2 * OCC - 2, 1), pl.ds(0, 2 * OCC - 1))[role]

    def is_kept(d):
        return group(d) % 2 == core

    def to_core(d, role):
        at = part_of(role)
        return remote(
            sums.at[slot(d), at], from_core.at[d // 2, at], c_s.at[d // 2, role % 3], c_r.at[d // 2, role % 3], dev(core_=1 - core)
        )

    def to_x(d, role, h, act):
        at, g = part_of(role), group(d)
        z2, z1 = g // 4, (g // 2) % 2
        delta = 2 * differs(h, hx) + differs(z2, zx)

        @pl.when(delta > 0)
        def _():
            act(
                remote(
                    sums.at[slot(d), at, pl.ds(h * HALF_J, HALF_J)], from_x.at[delta - 1, z1, at],
                    x_s.at[d // 2, role % 3, h], x_r.at[delta - 1, z1], dev(hx_=h, zx_=z2),
                )
            )

    def reduce_core(d, role):
        @pl.when(jnp.logical_not(is_kept(d)))
        def _():
            to_core(d, role).start()

    def reduce_x(d, role):
        @pl.when(is_kept(d))
        def _():
            to_core(d, role).wait_recv()
            at = part_of(role)
            sums[slot(d), at] += from_core[d // 2, at]
            for h in range(2):
                to_x(d, role, h, lambda copy: copy.start())

    def over_five(act):
        lax.fori_loop(0, 5, lambda t, _: (act(t + 3 * (t // 3)), 0)[1], 0)

    last = group(4)
    j_mine = pl.ds(pl.multiple_of(hx * HALF_J, 8), HALF_J)
    j_theirs = pl.ds(pl.multiple_of((1 - hx) * HALF_J, 8), HALF_J)
    most = pl.ds(0, OCC - 1)

    def unit(z1):
        return zx * 4 + z1 * 2 + core

    def kept_of(far):
        return most if far else pl.ds(0, OCC)

    def x_arrives(z1):
        for delta in range(3):
            place = from_x.at[delta, z1]
            remote(place, place, x_s.at[0, 0, 0], x_r.at[delta, z1], dev(hx_=1 - hx)).wait_recv()

    def x_sum(z1, far):
        at = pl.ds(OCC, OCC - 1) if far else pl.ds(0, OCC)
        value = sums[slot((unit(z1) - z + RING) % RING), at, j_mine, :]
        for delta in range(3):
            value = value + from_x[delta, z1, at]
        return value

    def y_copy(e):
        at = kept_of(e & 1)
        target = dev(yh_=1 - yh if e & 2 else yh, y_=1 - y if e & 1 else y)
        return remote(to_y.at[e - 1, at], from_y.at[e - 1, at], y_s.at[e - 1], y_r.at[e - 1], target)

    def y_send(e):
        to_y[e - 1, kept_of(e & 1)] = x_sum(1 - yh if e & 2 else yh, e & 1)
        y_copy(e).start()

    def y_stage():
        @pl.when(unit(1 - yh) != last)
        def _():
            x_arrives(1 - yh)
            y_send(2)
            y_send(3)

        @pl.when(unit(yh) != last)
        def _():
            x_arrives(yh)
            y_send(1)
            total[...] = x_sum(yh, 0)

    def y_sent():
        @pl.when(unit(1 - yh) != last)
        def _():
            y_copy(2).wait_send()
            y_copy(3).wait_send()

        @pl.when(unit(yh) != last)
        def _():
            y_copy(1).wait_send()

    def to_last(h, far):
        at = pl.ds(OCC, OCC - 1) if far else pl.ds(0, OCC)
        sender = y * RING + col // 2
        z2, z1 = last // 4, (last // 2) % 2
        target = dev(y_=1 - y if far else y, hx_=h, zx_=z2, yh_=z1)
        return remote(
            sums.at[slot(4), at, pl.ds(h * HALF_J, HALF_J)], from_last.at[sender, kept_of(far)],
            last_s.at[h, far], last_r.at[sender], target,
        )

    def each_last(act):
        for far in (1, 0):
            for h in range(2):
                if far:
                    act(to_last(h, far))
                else:

                    @pl.when(jnp.logical_not(jnp.logical_and(unit(yh) == last, h == hx)))
                    def _(h=h, far=far):
                        act(to_last(h, far))

    def reduce_last():
        @pl.when(is_kept(4))
        def _():
            to_core(4, 3).wait_recv()
            at = part_of(3)
            sums[slot(4), at] += from_core[2, at]
            each_last(lambda copy: copy.start())

    def last_sums():
        value = sums[slot(4), pl.ds(0, OCC), j_mine, :]
        total[...] = value

        def add(t, _):
            @pl.when(2 * t + core != col)
            def _():
                place = from_last.at[y * RING + t]
                remote(place, place, last_s.at[0, 0], last_r.at[y * RING + t], dev(hx_=1 - hx)).wait_recv()
                total[...] += from_last[y * RING + t]

            there = (1 - y) * RING + t
            place = from_last.at[there, most]
            remote(place, place, last_s.at[0, 0], last_r.at[there], dev(hx_=1 - hx)).wait_recv()
            total[most] += from_last[there, most]
            return 0

        lax.fori_loop(0, RING, add, 0)

    mirror = dev(hx_=1 - hx)

    def direct(k):
        at = pl.ds(OCC - 1, 1) if k else most
        return remote(total.at[at], direct_half.at[at], d_s.at[k], d_r.at[k], mirror)

    def mirror_copy(k, t, h):
        src, dst, send, recv = ((to_mirror, from_mirror, m_s, m_r), (to_late, from_late, lm_s, lm_r))[k]
        return remote(src.at[t], dst.at[row], send.at[t, h], recv.at[row], dev(hx_=h, y_=hx, z_=t))

    def each_mirror(act):
        def body(step, _):
            t = (z + RING // 2 + step) % RING
            for h in range(2):

                @pl.when(jnp.logical_not(is_me(h, hx, t)))
                def _():
                    act(t, h)

            return 0

        lax.fori_loop(0, RING, body, 0)

    def mirror_arrives(k):
        dst, send, recv = ((from_mirror, m_s, m_r), (from_late, lm_s, lm_r))[k]

        def body(r, _):
            @pl.when(jnp.logical_not(is_me(y, r // RING, r % RING)))
            def _():
                place = dst.at[r]
                remote(place, place, send.at[0, 0], recv.at[r], mirror).wait_recv()

            return 0

        lax.fori_loop(0, 2 * RING, body, 0)

    def spread():
        direct(0).start()
        for t in range(RING):
            for b in range(OCC):
                to_mirror[t, pl.ds(b * 4, 4), :] = total[most, t * OCC + b, :]
        each_mirror(lambda t, h: mirror_copy(0, t, h).start())

        @pl.when(hx == y)
        def _():
            from_mirror[row] = to_mirror[z]

    kept = (z + core) % 2
    late_core = remote(
        sums.at[pl.ds(4 * (1 - kept), 4), 2 * OCC - 1], late_in, lc_s, lc_r, dev(core_=1 - core)
    )

    def to_owner(q, h):
        d = 2 * q + kept
        src = sums.at[slot(d), 2 * OCC - 1, pl.ds(h * HALF_J, HALF_J)]
        owner = h * RING + group(d)
        return remote(src, from_all.at[col // 2], all_s.at[q, h], all_r.at[col // 2], ((1 - y) * RING + z, owner))

    def each_owner(act):
        def body(step, _):
            q = (step + col // 4) % (RING // 2)
            for h in range(2):
                act(to_owner(q, h))
            return 0

        lax.fori_loop(0, RING // 2, body, 0)

    product(0, OCC, slot(0), 1)
    reduce_core(0, 0)
    for n in range(STEPS - 2):
        if n == 4:
            for k in pieces(5):
                down(5, k).start()
        for u in pieces(n):
            up_arrives(n, u)
            if n + 2 < STEPS - 2:
                up(n + 2, u).start()
            down_arrives(n, u)
            if n in (0, 1):
                down(n + 2, u).start()
            elif n == 3:
                down(4, u).start()
        if n == 3:
            for k in pieces(5):
                up(5, k).start()
        elif n == 4:
            for k in pieces(6):
                up(6, k).start()
                down(6, k).start()
        if n == 1:
            swap_a(2).start()
        elif n in (2, 3):
            for k in range(len(cuts)):
                swap_cut(n + 1, k).start()
        if n == 0:
            reduce_x(0, 0)
        elif n in (1, 3):
            d = (n + 1) // 2
            for distance in (d, RING - d):
                product(0, OCC + d - 1, slot(distance), 1)
                reduce_core(distance, 0)
            for distance in (d, RING - d):
                reduce_x(distance, 0)
        if n == 2:
            swap_a(0).wait_recv()
            for distance in (0, 1, 7):
                product(OCC, 1, slot(distance), 1)
        elif n == 3:
            swap_a(1).wait_recv()
            five_blocks(OCC + 1)
        elif n == 4:
            swap_a(2).wait_recv()
            five_blocks(OCC + 2)
            over_five(lambda d: reduce_core(d, 1))
            over_five(lambda d: reduce_x(d, 1))

    def ring_sent(steps):
        for m in steps:
            for u in pieces(m):
                up(m, u).wait_send()
                down(m, u).wait_send()

    def sums_sent(d, role):
        @pl.when(jnp.logical_not(is_kept(d)))
        def _():
            to_core(d, role).wait_send()

        @pl.when(is_kept(d))
        def _():
            if isinstance(d, int) and d == 4:
                each_last(lambda copy: copy.wait_send())
            else:
                for h in range(2):
                    to_x(d, role, h, lambda copy: copy.wait_send())

    for u in range(SUB):
        swap_i(u).wait_send()
    ring_sent(range(4))
    for i in range(2):
        swap_a(i).wait_send()

    for k in range(len(cuts)):
        up_arrives(5, k)
        down_arrives(5, k)
        swap_cut(3, k).wait_recv()
        product(0, 2 * OCC - 1, slot(3), 2, k)
        five_blocks(2 * OCC - 2, k)
    for d in (3, 5):
        reduce_core(d, 3)
    over_five(lambda d: reduce_core(d, 2))
    for d in (3, 5):
        reduce_x(d, 3)
    over_five(lambda d: reduce_x(d, 2))

    ring_sent((4,))
    swap_a(2).wait_send()
    for role in range(2):
        over_five(lambda d, role=role: sums_sent(d, role))

    final = len(cuts) - 1
    for k in range(len(cuts)):
        up_arrives(6, k)
        down_arrives(6, k)
        product(0, 2 * OCC - 1, slot(4), 1, k)
        if k == 0:
            y_stage()
        if k == final:
            reduce_core(4, 3)
        for late in {0: (0,), final: range(1, final)}.get(k, ()):
            swap_cut(4, late).wait_recv()
            product(2 * OCC - 1, 1, 0, 4, late)
            product(2 * OCC - 1, 1, 4, 4, late)
    reduce_last()
    swap_cut(4, final).wait_recv()
    product(2 * OCC - 1, 1, 4 * (1 - kept), 4, final)
    late_core.start()
    product(2 * OCC - 1, 1, 4 * kept, 4, final)
    late_core.wait_recv()
    sums[pl.ds(4 * kept, 4), 2 * OCC - 1] += late_in[...]
    each_owner(lambda copy: copy.start())

    @pl.when(unit(yh) != last)
    def _():
        for e in (2, 3, 1):
            y_copy(e).wait_recv()
        total[...] += from_y[1]
        total[most] += from_y[0, most] + from_y[2, most]
        spread()

    @pl.when(unit(yh) == last)
    def _():
        last_sums()
        spread()

    def late_arrives(r, _):
        place = from_all.at[r]
        remote(place, place, all_s.at[0, 0], all_r.at[r], mirror).wait_recv()
        return 0

    lax.fori_loop(0, RING, late_arrives, 0)
    value = total[OCC - 1]
    for r in range(RING):
        value = value + from_all[r]
    total[OCC - 1] = value
    for t in range(RING):
        to_late[t, pl.ds(0, OCC), :] = total[OCC - 1, pl.ds(t * OCC, OCC), :]
    each_mirror(lambda t, h: mirror_copy(1, t, h).start())
    direct(1).start()

    @pl.when(hx == y)
    def _():
        from_late[row] = to_late[z]

    ring_sent((5, 6))
    for k in range(len(cuts)):
        swap_cut(3, k).wait_send()
        swap_cut(4, k).wait_send()
    over_five(lambda d: sums_sent(d, 2))
    for d in (3, 4, 5):
        sums_sent(d, 3)

    late_core.wait_send()
    each_owner(lambda copy: copy.wait_send())
    y_sent()
    mirror_arrives(0)
    for r in range(2 * RING):
        for b in range(OCC):
            turned[b, pl.ds(r * OCC, OCC - 1), :] = from_mirror[r, pl.ds(b * 4, 4), :]
    direct(0).wait_recv()

    direct(0).wait_send()
    each_mirror(lambda t, h: mirror_copy(0, t, h).wait_send())
    direct(1).wait_send()
    each_mirror(lambda t, h: mirror_copy(1, t, h).wait_send())
    mirror_arrives(1)
    for r in range(2 * RING):
        turned[:, r * OCC + OCC - 1, :] = from_late[r, pl.ds(0, OCC), :]
    direct(1).wait_recv()

    def finish(straight, swapped):
        straight, swapped = (v.reshape(OCC * HALF_J, LANES) for v in (straight, swapped))
        here = jnp.where(hx == 0, straight, swapped)
        there = jnp.where(hx == 0, swapped, straight)
        value = here + pltpu.roll(there, BLOCK, 1)
        return [value[i * HALF_J : (i + 1) * HALF_J] for i in range(OCC)]

    for h, straight in ((hx, total), (1 - hx, direct_half)):
        at = pl.ds(pl.multiple_of(h * HALF_J, 8), HALF_J)
        for i, value in enumerate(finish(straight[...], turned[:, at, :])):
            upright[pl.ds(pl.multiple_of(i * NOCC + h * HALF_J, 8), HALF_J), :] = value
    out[...] = upright[...].T[:BLOCK, : OCC * NOCC]


def on_device(amplitudes, integrals, residual_in):
    pairs, depth = amplitudes.shape
    half = depth // 2
    bf16, f32 = jnp.bfloat16, jnp.float32
    dma = pltpu.SemaphoreType.DMA
    cuts = len(CUTS) - 1
    ladder = pl.pallas_call(
        kernel,
        out_shape=jax.ShapeDtypeStruct((BLOCK, pairs), f32),
        in_specs=[pl.BlockSpec(memory_space=pltpu.HBM)] * 2,
        out_specs=pl.BlockSpec(memory_space=pltpu.VMEM),
        scratch_shapes=[
            pltpu.VMEM((2 * pairs, half), bf16),
            pltpu.VMEM((RING, LANES, half), bf16),
            pltpu.VMEM((RING, 2 * OCC, NOCC, LANES), f32),
            pltpu.VMEM((RING // 2, 2 * OCC - 1, NOCC, LANES), f32),
            pltpu.VMEM((3, 2, 2 * OCC - 1, HALF_J, LANES), f32),
            pltpu.VMEM((RING // 2, NOCC, LANES), f32),
            pltpu.VMEM((RING, HALF_J, LANES), f32),
            pltpu.VMEM((2 * RING, OCC, HALF_J, LANES), f32),
            pltpu.VMEM((3, OCC, HALF_J, LANES), f32),
            pltpu.VMEM((3, OCC, HALF_J, LANES), f32),
            pltpu.VMEM((OCC, HALF_J, LANES), f32),
            pltpu.VMEM((RING, 24, LANES), f32),
            pltpu.VMEM((2 * RING, 24, LANES), f32),
            pltpu.VMEM((RING, 8, LANES), f32),
            pltpu.VMEM((2 * RING, 8, LANES), f32),
            pltpu.VMEM((OCC, HALF_J, LANES), f32),
            pltpu.VMEM((OCC, NOCC, LANES), f32),
            pltpu.VMEM((4 * LANES, LANES), f32),
            dma((2,)),
            dma((SUB,)),
            dma((SUB,)),
            dma((OCC - 2,)),
            dma((OCC - 2,)),
            dma((2, cuts)),
            dma((2, cuts)),
            dma((STEPS, cuts)),
            dma((STEPS, cuts)),
            dma((STEPS, cuts)),
            dma((STEPS, cuts)),
            dma((RING // 2, 3)),
            dma((RING // 2, 3)),
            dma((RING // 2, 3, 2)),
            dma((3, 2)),
            dma,
            dma,
            dma((RING // 2, 2)),
            dma((RING,)),
            dma((2, 2)),
            dma((2 * RING,)),
            dma((3,)),
            dma((3,)),
            dma((RING, 2)),
            dma((2 * RING,)),
            dma((RING, 2)),
            dma((2 * RING,)),
            dma((2,)),
            dma((2,)),
        ],
        compiler_params=pltpu.CompilerParams(
            collective_id=0, has_side_effects=True, vmem_limit_bytes=53 * 1024 * 1024
        ),
        cost_estimate=pl.CostEstimate(
            flops=2 * pairs * depth * 16 * BLOCK, bytes_accessed=4 * pairs * depth, transcendentals=0
        ),
        name="ladder",
    )(amplitudes, integrals)
    return residual_in + ladder


def solution(mesh):
    placed = (P("row", "col"), P("row", "col"), P("col", "row"))
    return jax.shard_map(
        on_device, mesh=mesh, in_specs=placed, out_specs=P("col", "row"), check_vma=False
    )
```
